128 devices in a mesh: rep: 16 (over x, z_hi, core), fsdp: 8 (over z_lo, y).
Axes of the slice: x: 4, y: 4, z: 4 (z_hi: 2, z_lo: 2; z = z_hi * 2 + z_lo), core: 2. Of those that a mesh axis runs over, the one named last changes fastest.
Arguments:
- tokens: bfloat16 [65536, 640], P(('rep', 'fsdp')), may hold values from -6 to 6
- positions: int32 [65536], P(('rep', 'fsdp')), may hold values from 0 to 3583, as said below
- cotangent: bfloat16 [65536, 640], P(('rep', 'fsdp')), may hold values from -6 to 6
- query_weight: bfloat16 [640, 1024], P('fsdp'), may hold values from -0.25 to 0.25
- key_weight: bfloat16 [640, 256], P('fsdp'), may hold values from -0.25 to 0.25
- value_weight: bfloat16 [640, 256], P('fsdp'), may hold values from -0.25 to 0.25
- output_weight: bfloat16 [1024, 640], P('fsdp'), may hold values from -0.75 to 0.75
- gate_weight: bfloat16 [640, 2048], P('fsdp'), may hold values from -0.25 to 0.25
- upward_weight: bfloat16 [640, 2048], P('fsdp'), may hold values from -0.25 to 0.25
- down_weight: bfloat16 [2048, 640], P('fsdp'), may hold values from -0.125 to 0.125
- gain_input: bfloat16 [640], P('fsdp'), may hold values from 0.099609375 to 1.8984375
- gain_mixed: bfloat16 [640], P('fsdp'), may hold values from 0.099609375 to 1.8984375
- gain_hidden: bfloat16 [640], P('fsdp'), may hold values from 0.099609375 to 1.8984375
- gain_final: bfloat16 [640], P('fsdp'), may hold values from 0.099609375 to 1.8984375
- gain_query: bfloat16 [256], P('fsdp'), may hold values from 0.099609375 to 1.8984375
- gain_key: bfloat16 [256], P('fsdp'), may hold values from 0.099609375 to 1.8984375
Outputs:
- layer_out: float32 [65536, 640], P(('rep', 'fsdp'))
- grad_tokens: float32 [65536, 640], P(('rep', 'fsdp'))
- grad_query_weight: float32 [640, 1024], P('fsdp')
- grad_key_weight: float32 [640, 256], P('fsdp')
- grad_value_weight: float32 [640, 256], P('fsdp')
- grad_output_weight: float32 [1024, 640], P('fsdp')
- grad_gate_weight: float32 [640, 2048], P('fsdp')
- grad_upward_weight: float32 [640, 2048], P('fsdp')
- grad_down_weight: float32 [2048, 640], P('fsdp')
- grad_gain_input: float32 [640], P('fsdp')
- grad_gain_mixed: float32 [640], P('fsdp')
- grad_gain_hidden: float32 [640], P('fsdp')
- grad_gain_final: float32 [640], P('fsdp')
- grad_gain_query: float32 [256], P('fsdp')
- grad_gain_key: float32 [256], P('fsdp')
The draws below stay inside these ranges and needn't reach their ends.
Inputs may be any that keep to these rules, and one draw needn't show every extreme that they name: `positions`: along each sequence of 4096 consecutive tokens a position is 0 or one more than the position of the token before it, and a sequence's first token has position 0. Each sequence holds one document of 3584 tokens that begins within its first 512 tokens; the tokens before it form one document, those after it one or two.
All inputs are finite; a program needn't handle non-finite values.
Results may differ from the reference program's by a relative error of at most 0.025.
Values may be sent and summed in bfloat16 or wider, within the bound.
No kernel may reach another device: no remote copies, remote signals or barrier semaphores. Data moves between devices by JAX's collectives and lax.ppermute only.
A program may use at most 128 MiB of HBM per device.

```python
import jax
import jax.numpy as jnp
from jax import lax

D = 640
FF = 2048
HEADS = 4
HEAD = 256
WINDOW = 512
TOK_DEV = 512
SEQ_LEN = 4096
SEQS = 16
TOKENS = 65536


def draw_positions(key, part):
    seq_keys = jax.random.split(jax.random.fold_in(key, 11), SEQS)

    def one_sequence(seq_key):
        key_start, key_cut = jax.random.split(seq_key, 2)
        start = jax.random.randint(key_start, (), 1, TOK_DEV)
        after = start + SEQ_LEN - TOK_DEV
        cut = jax.random.randint(key_cut, (), after, SEQ_LEN)
        index = jnp.arange(SEQ_LEN, dtype=jnp.int32)
        bounds = (index == 0) | (index == start) | (index == after) | (index == cut)
        latest = lax.cummax(jnp.where(bounds, index, 0), axis=0)
        return index - latest
    return jax.vmap(one_sequence)(seq_keys).reshape(-1).astype(jnp.int32)


def shard_levels(key, dims, pieces, smallest, largest):
    def one(axis_at, parts):
        steps = jax.random.uniform(jax.random.fold_in(jax.random.fold_in(key, 6), axis_at), (parts,), jnp.float32, smallest / len(pieces), largest / len(pieces))
        return jnp.repeat(jnp.exp(steps), dims[axis_at] // parts).reshape((-1,) + (1,) * (len(dims) - axis_at - 1))

    level = one(*pieces[0])
    for cut in pieces[1:]:
        level = level * one(*cut)
    return level


def gaussian(stream_key, extent, scale, most, cuts=(), kind=jnp.bfloat16):
    factor_of = shard_levels(stream_key, extent, cuts, -0.22, 0.18) if cuts else 1.0
    values = jax.random.normal(stream_key, extent, jnp.float32) * scale * factor_of
    return jnp.minimum(jnp.maximum(values, -most), most).astype(kind)


def setup_inputs(seed: int = 0) -> dict:
    splits = jax.random.split(jax.random.key(seed), 17)
    tokens = gaussian(splits[0], (TOKENS, D), 1.0, 6.0, ((0, 128),))
    positions = draw_positions(jax.random.fold_in(splits[16], 71), 0)
    cotangent = gaussian(splits[2], (TOKENS, D), 1.0, 6.0, ((0, 128),))
    query_weight = gaussian(splits[3], (D, HEADS * HEAD), D ** -0.5, 0.25, ((0, 8),))
    key_weight = gaussian(splits[4], (D, HEAD), D ** -0.5, 0.25, ((0, 8),))
    value_weight = gaussian(splits[5], (D, HEAD), D ** -0.5, 0.25, ((0, 8),))
    output_weight = gaussian(splits[6], (HEADS * HEAD, D), (HEADS * HEAD // 16) ** -0.5, 0.75, ((0, 8),))
    gate_weight = gaussian(splits[7], (D, FF), D ** -0.5, 0.25, ((0, 8),))
    upward_weight = gaussian(splits[8], (D, FF), D ** -0.5, 0.25, ((0, 8),))
    down_weight = gaussian(splits[9], (FF, D), FF ** -0.5, 0.125, ((0, 8),))
    gain_input = jnp.clip(1.0 + 0.18 * jax.random.normal(splits[10], (D,), jnp.float32), 0.099609375, 1.8984375).astype(jnp.bfloat16)
    gain_mixed = jnp.clip(1.0 + 0.18 * jax.random.normal(splits[11], (D,), jnp.float32), 0.099609375, 1.8984375).astype(jnp.bfloat16)
    gain_hidden = jnp.clip(1.0 + 0.18 * jax.random.normal(splits[12], (D,), jnp.float32), 0.099609375, 1.8984375).astype(jnp.bfloat16)
    gain_final = jnp.clip(1.0 + 0.18 * jax.random.normal(splits[13], (D,), jnp.float32), 0.099609375, 1.8984375).astype(jnp.bfloat16)
    gain_query = jnp.clip(1.0 + 0.18 * jax.random.normal(splits[14], (HEAD,), jnp.float32), 0.099609375, 1.8984375).astype(jnp.bfloat16)
    gain_key = jnp.clip(1.0 + 0.18 * jax.random.normal(splits[15], (HEAD,), jnp.float32), 0.099609375, 1.8984375).astype(jnp.bfloat16)
    return {"tokens": tokens, "positions": positions, "cotangent": cotangent, "query_weight": query_weight, "key_weight": key_weight, "value_weight": value_weight, "output_weight": output_weight, "gate_weight": gate_weight, "upward_weight": upward_weight, "down_weight": down_weight, "gain_input": gain_input, "gain_mixed": gain_mixed, "gain_hidden": gain_hidden, "gain_final": gain_final, "gain_query": gain_query, "gain_key": gain_key}


EPS = 1e-06
THETA = 10000.0
SCALE = 0.0625
NEG = -1e+30
HIGH = lax.Precision.HIGHEST

@jax.custom_vjp
def low(v):
    return lax.optimization_barrier(v.astype(jnp.bfloat16)).astype(jnp.float32)

@jax.custom_vjp
def low_back(v):
    return v

def low_keep(v):
    return (low(v), None)

def low_pass(kept, grad):
    return (grad,)

def back_keep(v):
    return (v, None)

def back_low(kept, grad):
    return (low(grad),)
low.defvjp(low_keep, low_pass)
low_back.defvjp(back_keep, back_low)

def matmul(left, right):
    return jnp.dot(left, right, preferred_element_type=jnp.float32, precision=HIGH)

def norm(values, gain):
    return values * lax.rsqrt(lax.optimization_barrier(jnp.mean(values * values, axis=-1, keepdims=True)) + EPS) * gain

def rotate(values, cosine, sine):
    half = values.shape[-1] // 2
    first = values[..., :half]
    second = values[..., half:]
    return jnp.concatenate([first * cosine - second * sine, second * cosine + first * sine], axis=-1)

def angles(positions):
    freqs = THETA ** (-(jnp.arange(HEAD // 2, dtype=jnp.float32) * 2.0) / HEAD)
    phase = positions.astype(jnp.float32)[:, None] * freqs[None, :]
    return (jnp.cos(phase), jnp.sin(phase))

def attend(queries, keys, values, positions):
    length = queries.shape[0]
    block = min(512, length)
    pad_keys = jnp.pad(keys, ((WINDOW, 0), (0, 0)))
    pad_values = jnp.pad(values, ((WINDOW, 0), (0, 0)))

    def one_block(start):
        rows = lax.dynamic_slice_in_dim(queries, start, block, 0)
        where_doc = lax.dynamic_slice_in_dim(positions, start, block, 0)
        near_keys = lax.dynamic_slice_in_dim(pad_keys, start, block + WINDOW, 0)
        near_values = lax.dynamic_slice_in_dim(pad_values, start, block + WINDOW, 0)
        query_index = start + jnp.arange(block, dtype=jnp.int32)
        key_index = start - WINDOW + jnp.arange(block + WINDOW, dtype=jnp.int32)
        doc_start = query_index - where_doc
        allowed = (key_index[None, :] <= query_index[:, None]) & (query_index[:, None] - key_index[None, :] < WINDOW) & (key_index[None, :] >= doc_start[:, None])
        scores = low_back(jnp.einsum('qhd,kd->hqk', rows, near_keys, precision=HIGH) * SCALE)
        scores = jnp.where(allowed[None], scores, NEG)
        row_max = lax.optimization_barrier(jnp.max(scores, axis=-1, keepdims=True))
        expd = jnp.exp(scores - row_max)
        probs = low(expd / lax.optimization_barrier(jnp.sum(expd, axis=-1, keepdims=True)))
        return jnp.einsum('hqk,kd->qhd', probs, near_values, precision=HIGH)
    starts = jnp.arange(length // block, dtype=jnp.int32) * block
    blocks = lax.map(jax.checkpoint(one_block), starts)
    return blocks.reshape(length, queries.shape[1] * queries.shape[2])

def forward(inputs, weights, positions):
    query_mat, key_mat, value_mat, out_mat, gate_mat, up_mat, down_mat, g_input, g_mixed, g_hidden, g_final, g_query, g_key = weights
    length = inputs.shape[0]
    cosine, sine = angles(positions)
    normed_in = low(norm(inputs, g_input))
    query_raw = low_back(matmul(normed_in, query_mat)).reshape(length, HEADS, HEAD)
    key_raw = low_back(matmul(normed_in, key_mat))
    values = low(low_back(matmul(normed_in, value_mat)))
    queries = low(rotate(norm(query_raw, g_query), cosine[:, None, :], sine[:, None, :]))
    keys = low(rotate(norm(key_raw, g_key), cosine, sine))
    mixed = low(low_back(attend(queries, keys, values, positions)))
    branch = low_back(matmul(mixed, out_mat))
    middle = inputs + norm(branch, g_mixed)
    normed_mid = low(norm(middle, g_hidden))
    gate = low_back(matmul(normed_mid, gate_mat))
    upward = low_back(matmul(normed_mid, up_mat))
    hidden = low(jax.nn.gelu(gate, approximate=True) * upward)
    down = low_back(matmul(hidden, down_mat))
    return middle + norm(down, g_final)

def reference(tokens, positions, cotangent, query_weight, key_weight, value_weight, output_weight, gate_weight, upward_weight, down_weight, gain_input, gain_mixed, gain_hidden, gain_final, gain_query, gain_key):
    weights = (query_weight.astype(jnp.float32), key_weight.astype(jnp.float32), value_weight.astype(jnp.float32), output_weight.astype(jnp.float32), gate_weight.astype(jnp.float32), upward_weight.astype(jnp.float32), down_weight.astype(jnp.float32), gain_input.astype(jnp.float32), gain_mixed.astype(jnp.float32), gain_hidden.astype(jnp.float32), gain_final.astype(jnp.float32), gain_query.astype(jnp.float32), gain_key.astype(jnp.float32))
    seq_inputs = tokens.astype(jnp.float32).reshape(SEQS, SEQ_LEN, D)
    seq_positions = positions.astype(jnp.int32).reshape(SEQS, SEQ_LEN)
    seq_grads = cotangent.astype(jnp.float32).reshape(SEQS, SEQ_LEN, D)

    def one_sequence(totals, item):
        inputs, where_doc, upstream = item

        def apply(values_in, params):
            return forward(values_in, params, where_doc)
        result, pull = jax.vjp(apply, inputs, weights)
        grad_in, grad_params = pull(upstream)
        summed = jax.tree.map(lambda total, grad: total + grad, totals, grad_params)
        return (summed, (result, grad_in))
    zeros = jax.tree.map(jnp.zeros_like, weights)
    totals, (results, grad_inputs) = lax.scan(one_sequence, zeros, (seq_inputs, seq_positions, seq_grads))
    return (results.reshape(TOKENS, D), grad_inputs.reshape(TOKENS, D), totals[0], totals[1], totals[2], totals[3], totals[4], totals[5], totals[6], totals[7], totals[8], totals[9], totals[10], totals[11], totals[12])
```

```python
import jax
import jax.numpy as jnp
from jax import lax
from jax.experimental import pallas as pl
from jax.experimental.pallas import tpu as pltpu
from jax.sharding import Mesh
from jax.sharding import PartitionSpec as P

HEADS = 4
HEAD = 256
WINDOW = 512
ROWS = 512
EPS = 1e-06
THETA = 10000.0
SCALE = 0.0625
NEG = -1e30
GELU_A = 0.7978845608028654
GELU_B = 0.044715

REP = ("x", "zh", "core")
FSDP = ("zl", "y")
BF16 = jnp.bfloat16
F32 = jnp.float32
ANY = pl.BlockSpec(memory_space=pl.ANY)
VMEM = pl.BlockSpec(memory_space=pltpu.VMEM)
SMEM = pl.BlockSpec(memory_space=pltpu.SMEM)


def shape(dims, dtype):
    return jax.ShapeDtypeStruct(dims, dtype)


def call(kernel, ins, in_specs, outs, scratch=(), flops=0):
    size = sum(a.size * a.dtype.itemsize for a in ins)
    size += sum(o.size * o.dtype.itemsize for o in outs)
    return pl.pallas_call(
        kernel,
        out_shape=outs,
        in_specs=in_specs,
        out_specs=[VMEM] * len(outs),
        scratch_shapes=list(scratch),
        compiler_params=pltpu.CompilerParams(vmem_limit_bytes=60 * 1024 * 1024),
        cost_estimate=pl.CostEstimate(flops=1, bytes_accessed=1, transcendentals=0),
    )(*ins)


def passed_along(value, steps):
    initial, last = (max(0, -steps), min(8, 8 - steps))
    pairs = [(source, source + steps) for source in range(initial, last)]
    return lax.ppermute(value, FSDP, pairs)


def swapped(value):
    return lax.ppermute(value, "core", [(0, 1), (1, 0)])


def along_y(spread):
    return lax.all_to_all(spread, "y", 0, 0, tiled=True)


def gathered(near, steps):
    far = lax.ppermute(near, ("zh", "zl"), [(i, (i + steps) % 4) for i in range(4)])
    return near, far, swapped(near), swapped(far)


def after(value, earlier):
    return lax.optimization_barrier((value, earlier))[0]


def pair_sum(own, other):
    return (own.astype(F32) + swapped(other).astype(F32)).astype(BF16)


def chips_sum(both):
    parts = lax.all_to_all(both, ("zl", "y", "x", "zh"), 0, 0, tiled=True)
    return jnp.sum(parts.astype(F32), axis=0).astype(BF16)


def normalize(values):
    factor = lax.rsqrt(jnp.mean(values * values, axis=-1, keepdims=True) + EPS)
    return (values * factor, factor)


def norm_back(grad_hat, unit, factor):
    return factor * (grad_hat - unit * jnp.mean(grad_hat * unit, axis=-1, keepdims=True))


def rotate(values, cosine, sine):
    first, second = values[:, :128], values[:, 128:]
    return jnp.concatenate(
        [first * cosine - second * sine, second * cosine + first * sine], axis=-1
    )


def product(left, right):
    return jnp.dot(left, right, preferred_element_type=F32)


def product_rt(left, right):
    return lax.dot_general(left, right, (((1,), (1,)), ((), ())), preferred_element_type=F32)


def product_lt(left, right):
    return lax.dot_general(left, right, (((0,), (0,)), ((), ())), preferred_element_type=F32)


def column_sum(values):
    return jnp.sum(values, axis=0, keepdims=True)


def load_pieces(pieces, target, core, zl, sems):
    copies = []
    for i, piece in enumerate(pieces):
        half = core if i < 2 else 1 - core
        group = zl if i % 2 == 0 else 1 - zl
        copies.append(
            pltpu.make_async_copy(piece, target.at[half, pl.ds(group * 4, 4)], sems.at[i])
        )
    for copy in copies:
        copy.start()
    return copies


def early_kernel(sc_ref, query_ref, key_ref, value_ref, gains_ref, out_ref):
    core, member = sc_ref[0], sc_ref[2]
    for c, last in enumerate((key_ref, value_ref)):

        @pl.when(core == c)
        def _():
            for k in range(4):
                out_ref[k, 0:80, 0:512] = query_ref[:, 512 * c : 512 * c + 512]
                out_ref[k, 0:80, 512:768] = last[...]

    padded = jnp.concatenate([gains_ref[...], jnp.zeros((8, 640), F32)], axis=1)
    model = pltpu.roll(padded, member * 80, 1)
    head = pltpu.roll(padded, member * 32, 1)
    which = lax.broadcasted_iota(jnp.int32, (8, 768), 0)
    rows = jnp.concatenate([jnp.where(which < 4, model, head), jnp.zeros((8, 768), F32)], axis=0)
    for k in range(4):
        out_ref[k, 80:96, :] = rows.astype(BF16)


def late_kernel(sc_ref, output_ref, down_ref, gate_ref, up_ref, tall_out, gate_out, up_out):
    core = sc_ref[0]
    for c in range(2):

        @pl.when(core == c)
        def _():
            for k in range(4):
                tall_out[k, 0:64, :] = output_ref[64 * c : 64 * c + 64, :]
                tall_out[k, 64:192, :] = down_ref[128 * c : 128 * c + 128, :]
                for f in range(8):
                    cols = slice(128 * f, 128 * f + 128)
                    source = slice(256 * f + 128 * c, 256 * f + 128 * c + 128)
                    gate_out[k, :, cols] = gate_ref[:, source]
                    up_out[k, :, cols] = up_ref[:, source]


def attend_kernel(
    sc_ref, tok_ref, prev_ref, cos_ref, sin_ref, pos_ref, near, far, near_t, far_t,
    q_ref, k_ref, v_ref, raw_ref, p_ref, mixed_ref, gains_ref, e_ref, sems,
):
    core, zl = sc_ref[0], sc_ref[1]
    copies = load_pieces((near, far, near_t, far_t), e_ref, core, zl, sems)
    unit, _ = normalize(tok_ref[...].astype(F32))
    unit_prev, _ = normalize(prev_ref[...].astype(F32))
    for copy in copies:
        copy.wait()
    gains = jnp.sum(e_ref[0, :, 80:96, :].astype(F32), axis=0)
    gains_ref[...] = gains
    normed = (unit * gains[0:1, :640]).astype(BF16)
    normed_prev = (unit_prev * gains[0:1, :640]).astype(BF16)
    g_query, g_key = gains[4:5, :256], gains[5:6, :256]
    mat_0 = e_ref[0, :, 0:80, :].reshape(640, 768)
    mat_1 = e_ref[1, :, 0:80, :].reshape(640, 768)
    raw_0 = product(normed, mat_0)
    raw_1 = product(normed, mat_1)
    raw_ref[:, 0:512] = raw_0[:, :512]
    raw_ref[:, 512:1024] = raw_1[:, :512]
    raw_ref[:, 1024:1280] = raw_0[:, 512:]
    v_ref[0:512, :] = product(normed_prev, mat_1[:, 512:]).astype(BF16)
    v_ref[512:1024, :] = raw_1[:, 512:].astype(BF16)
    prev_unit, _ = normalize(product(normed_prev, mat_0[:, 512:]))
    k_ref[0:512, :] = rotate(prev_unit * g_key, cos_ref[0:512, :], sin_ref[0:512, :]).astype(BF16)
    cosine, sine = cos_ref[512:1024, :], sin_ref[512:1024, :]
    own_unit, _ = normalize(raw_0[:, 512:])
    k_ref[512:1024, :] = rotate(own_unit * g_key, cosine, sine).astype(BF16)
    for h in range(HEADS):
        q_unit, _ = normalize(raw_ref[:, 256 * h : 256 * h + 256])
        turned = rotate(q_unit * g_query, cosine, sine).astype(BF16)
        q_ref[:, 256 * h : 256 * h + 256] = turned * BF16(SCALE)
    for b in range(2):
        rows = slice(256 * b, 256 * b + 256)
        keys = slice(256 * b, 256 * b + 768)
        query_at = lax.broadcasted_iota(jnp.int32, (256, 768), 0)
        key_at = lax.broadcasted_iota(jnp.int32, (256, 768), 1) - 512
        back = query_at - key_at
        allowed = (back >= 0) & (back < WINDOW) & (back <= pos_ref[rows, :])
        for h in range(HEADS):
            cols = slice(256 * h, 256 * h + 256)
            scores = jnp.where(allowed, product_rt(q_ref[rows, cols], k_ref[keys, :]), NEG)
            expd = jnp.exp(scores - jnp.max(scores, axis=-1, keepdims=True))
            probs = (expd / jnp.sum(expd, axis=-1, keepdims=True)).astype(BF16)
            p_ref[h, b] = probs
            mixed_ref[rows, cols] = product(probs, v_ref[keys, :]).astype(BF16)


def load_wide(pieces, target, zl, sems):
    copies = []
    for i, piece in enumerate(pieces):
        group = zl if i % 2 == 0 else 1 - zl
        place = target.at[i // 4, i // 2 % 2, pl.ds(group * 4, 4)]
        copies.append(pltpu.make_async_copy(piece, place, sems.at[i]))
    for copy in copies:
        copy.start()
    return copies


def load_tall(pieces, out_w, down_w, core, zl, sems):
    copies = []
    for i, piece in enumerate(pieces):
        half = core if i < 2 else 1 - core
        group = zl if i % 2 == 0 else 1 - zl
        members = pl.ds(group * 4, 4)
        copies.append(
            pltpu.make_async_copy(piece.at[:, 0:64], out_w.at[members, half], sems.at[2 * i])
        )
        copies.append(
            pltpu.make_async_copy(
                piece.at[:, 64:192], down_w.at[i // 2, members], sems.at[2 * i + 1]
            )
        )
    for copy in copies:
        copy.start()
    return copies


def forward_kernel(
    sc_ref, mixed_ref, tok_ref, cot_ref, gains_ref, w0, w1, w2, w3, w4, w5, w6, w7, t0, t1, t2, t3,
    out_ref, branch_ref, middle_ref, nm_ref, act_ref, slope_ref, gd_ref, own_ref, other_ref, gain_ref,
    wide_w, out_w, down_w, hid_ref, wide_sems, tall_sems,
):
    core, zl = sc_ref[0], sc_ref[1]
    tall = load_tall((t0, t1, t2, t3), out_w, down_w, core, zl, tall_sems)
    wide = load_wide((w0, w1, w2, w3, w4, w5, w6, w7), wide_w, zl, wide_sems)
    for copy in tall:
        copy.wait()
    g_mixed, g_hidden, g_final = [gains_ref[i : i + 1, :640] for i in (1, 2, 3)]
    out_mat = out_w[...].reshape(1024, 640)
    branch_ref[...] = product(mixed_ref[...], out_mat)
    for copy in wide:
        copy.wait()
    gain_sum = jnp.zeros((1, 640), F32)
    for b in range(2):
        rows = slice(256 * b, 256 * b + 256)
        branch_unit, _ = normalize(branch_ref[rows, :])
        middle = tok_ref[rows, :].astype(F32) + branch_unit * g_mixed
        middle_ref[rows, :] = middle
        mid_unit, _ = normalize(middle)
        normed = (mid_unit * g_hidden).astype(BF16)
        nm_ref[rows, :] = normed
        down = jnp.zeros((256, 640), F32)
        for half in range(2):
            for n in range(2):
                cols = slice(512 * n, 512 * n + 512)
                u = product(normed, wide_w[0, half, :, :, cols].reshape(640, 512))
                upward = product(normed, wide_w[1, half, :, :, cols].reshape(640, 512))
                square = u * u
                t = jnp.tanh(GELU_A * u * (1.0 + GELU_B * square))
                side = 0.5 * (1.0 + t)
                active = u * side
                slope = side + 0.5 * u * (1.0 - t * t) * (GELU_A * (1.0 + 3.0 * GELU_B * square))
                act_ref[half, rows, cols] = active.astype(BF16)
                slope_ref[half, rows, cols] = (slope * upward).astype(BF16)
                hidden = (active * upward).astype(BF16)
                hid_ref[half, rows, cols] = hidden
                mat = down_w[half, 4 * n : 4 * n + 4].reshape(512, 640)
                down = down + product(hidden, mat)
        down_unit, down_factor = normalize(down)
        out_ref[rows, :] = middle + down_unit * g_final
        grad_out = cot_ref[rows, :].astype(F32)
        gain_sum = gain_sum + column_sum(grad_out * down_unit)
        gd_ref[rows, :] = norm_back(grad_out * g_final, down_unit, down_factor).astype(BF16)
    gain_ref[...] = gain_sum
    for half, ref in enumerate((own_ref, other_ref)):
        for n in range(2):
            part = product_lt(hid_ref[half, :, 512 * n : 512 * n + 512], gd_ref[...])
            part = part.astype(BF16).reshape(4, 8, 16, 640)
            for j in range(5):
                ref[4 * n : 4 * n + 4, :, j] = part[:, :, :, 128 * j : 128 * j + 128]


def backward_kernel(
    sc_ref, mixed_ref, cot_ref, gains_ref, branch_ref, middle_ref, nm_ref, act_ref, slope_ref, gd_ref,
    w0, w1, w2, w3, w4, w5, w6, w7, t0, t1, t2, t3,
    gmid_ref, gmixed_ref, own_ref, other_ref, gain_ref,
    wide_w, out_w, down_w, gg_ref, gu_ref, gb_ref, split_ref, wide_sems, tall_sems,
):
    core, zl = sc_ref[0], sc_ref[1]
    tall = load_tall((t0, t1, t2, t3), out_w, down_w, core, zl, tall_sems)
    wide = load_wide((w0, w1, w2, w3, w4, w5, w6, w7), wide_w, zl, wide_sems)
    for copy in tall + wide:
        copy.wait()
    g_mixed, g_hidden = [gains_ref[i : i + 1, :640] for i in (1, 2)]
    sum_mixed = jnp.zeros((1, 640), F32)
    sum_hidden = jnp.zeros((1, 640), F32)
    for b in range(2):
        rows = slice(256 * b, 256 * b + 256)
        grad_normed = jnp.zeros((256, 640), F32)
        for half in range(2):
            for n in range(2):
                cols = slice(512 * n, 512 * n + 512)
                mat = down_w[half, 4 * n : 4 * n + 4].reshape(512, 640)
                grad_hidden = product_rt(gd_ref[rows, :], mat)
                grad_gate = (grad_hidden * slope_ref[half, rows, cols].astype(F32)).astype(BF16)
                grad_up = (grad_hidden * act_ref[half, rows, cols].astype(F32)).astype(BF16)
                gg_ref[half, rows, cols] = grad_gate
                gu_ref[half, rows, cols] = grad_up
                grad_normed = grad_normed + product_rt(
                    grad_gate, wide_w[0, half, :, :, cols].reshape(640, 512)
                )
                grad_normed = grad_normed + product_rt(
                    grad_up, wide_w[1, half, :, :, cols].reshape(640, 512)
                )
        mid_unit, mid_factor = normalize(middle_ref[rows, :])
        sum_hidden = sum_hidden + column_sum(grad_normed * mid_unit)
        grad_middle = cot_ref[rows, :].astype(F32) + norm_back(
            grad_normed * g_hidden, mid_unit, mid_factor
        )
        gmid_ref[rows, :] = grad_middle
        branch_unit, branch_factor = normalize(branch_ref[rows, :])
        sum_mixed = sum_mixed + column_sum(grad_middle * branch_unit)
        grad_branch = norm_back(grad_middle * g_mixed, branch_unit, branch_factor).astype(BF16)
        gb_ref[rows, :] = grad_branch
        gmixed_ref[rows, :] = product_rt(grad_branch, out_w[...].reshape(1024, 640)).astype(BF16)
    gain_ref[0:1, :] = sum_mixed
    gain_ref[1:2, :] = sum_hidden
    for half, ref in enumerate((own_ref, other_ref)):
        for at, grads in enumerate((gg_ref, gu_ref)):
            for n in range(2):
                part = product_lt(nm_ref[...], grads[half, :, 512 * n : 512 * n + 512])
                part = part.astype(BF16).reshape(8, 5, 16, 512)
                for j in range(4):
                    ref[:, 5 * at : 5 * at + 5, 4 * n + j] = part[:, :, :, 128 * j : 128 * j + 128]
    for n in range(2):
        part = product_lt(mixed_ref[:, 512 * n : 512 * n + 512], gb_ref[...])
        part = part.astype(BF16).reshape(4, 2, 4, 16, 640)
        for c in range(2):
            split_ref[c, 4 * n : 4 * n + 4] = part[:, c]
    for half, ref in ((core, own_ref), (1 - core, other_ref)):
        part = split_ref[half]
        for i in range(4):
            for j in range(5):
                at = i * 5 + j
                ref[:, 10 + at // 8, at % 8] = part[:, i, :, 128 * j : 128 * j + 128]
        ref[:, 12, 4:8] = jnp.zeros((8, 4, 16, 128), BF16)


def attend_back_kernel(
    q_ref, k_ref, v_ref, p_ref, gm_ref, gq_ref, far_k_ref, far_v_ref, own_k_ref, own_v_ref, dk_ref, dv_ref
):
    dk_ref[...] = jnp.zeros((1024, 256), F32)
    dv_ref[...] = jnp.zeros((1024, 256), F32)
    for b in range(2):
        rows = slice(256 * b, 256 * b + 256)
        keys = slice(256 * b, 256 * b + 768)
        for h in range(HEADS):
            cols = slice(256 * h, 256 * h + 256)
            probs = p_ref[h, b]
            grads = gm_ref[rows, cols]
            weighed = probs.astype(F32)
            grad_probs = product_rt(grads, v_ref[keys, :])
            inner = jnp.sum(weighed * grad_probs, axis=-1, keepdims=True)
            grad_scores = (weighed * (grad_probs - inner)).astype(BF16)
            gq_ref[rows, cols] = product(grad_scores, k_ref[keys, :]) * SCALE
            dk_ref[keys, :] += product_lt(grad_scores, q_ref[rows, cols])
            dv_ref[keys, :] += product_lt(probs, grads)
    far_k_ref[...] = dk_ref[0:512, :].astype(BF16)
    far_v_ref[...] = dv_ref[0:512, :].astype(BF16)
    own_k_ref[...] = dk_ref[512:1024, :]
    own_v_ref[...] = dv_ref[512:1024, :]


def query_back_kernel(gq_ref, raw_ref, cos_ref, sin_ref, gains_ref, e_ref, low_ref, gn_ref, gain_ref):
    cosine, sine = cos_ref[512:1024, :], sin_ref[512:1024, :]
    g_query = gains_ref[4:5, :256]
    total = jnp.zeros((1, 256), F32)
    for h in range(HEADS):
        cols = slice(256 * h, 256 * h + 256)
        turned = rotate(gq_ref[:, cols], cosine, -sine)
        unit, factor = normalize(raw_ref[:, cols])
        total = total + column_sum(turned * unit)
        low_ref[:, cols] = norm_back(turned * g_query, unit, factor).astype(BF16)
    gain_ref[...] = total
    gn_ref[...] = product_rt(
        low_ref[:, 0:512], e_ref[0, :, 0:80, 0:512].reshape(640, 512)
    ) + product_rt(low_ref[:, 512:1024], e_ref[1, :, 0:80, 0:512].reshape(640, 512))


def final_back_kernel(
    sc_ref, tok_ref, low_ref, gn_ref, own_k_ref, own_v_ref, back_k_ref, back_v_ref, raw_ref, cos_ref, sin_ref,
    gains_ref, e_ref, gmid_ref, gain_q_ref, gain_b_ref, gain_f_ref,
    gtok_ref, own_ref, other_ref, split_ref, rows_ref,
):
    core = sc_ref[0]
    cosine, sine = cos_ref[512:1024, :], sin_ref[512:1024, :]
    g_input, g_key = gains_ref[0:1, :640], gains_ref[5:6, :256]
    key_grad = own_k_ref[...] + back_k_ref[...].astype(F32)
    grad_values = (own_v_ref[...] + back_v_ref[...].astype(F32)).astype(BF16)
    turned = rotate(key_grad, cosine, -sine)
    unit, factor = normalize(raw_ref[:, 1024:1280])
    key_gain = column_sum(turned * unit)
    grad_key = norm_back(turned * g_key, unit, factor).astype(BF16)
    grad_normed = (
        gn_ref[...]
        + product_rt(grad_key, e_ref[0, :, 0:80, 512:768].reshape(640, 256))
        + product_rt(grad_values, e_ref[1, :, 0:80, 512:768].reshape(640, 256))
    )
    unit_in, factor_in = normalize(tok_ref[...].astype(F32))
    input_gain = column_sum(grad_normed * unit_in)
    gtok_ref[...] = gmid_ref[...] + norm_back(grad_normed * g_input, unit_in, factor_in)
    normed = (unit_in * g_input).astype(BF16)
    for c, last in enumerate((grad_key, grad_values)):
        for part, at in (
            (product_lt(normed, low_ref[:, 512 * c : 512 * c + 512]), 0),
            (product_lt(normed, last), 4),
        ):
            width = part.shape[1] // 128
            part = part.astype(BF16).reshape(8, 5, 16, part.shape[1])
            for i in range(5):
                for j in range(width):
                    split_ref[c, :, i * 6 + at + j] = part[:, i, :, 128 * j : 128 * j + 128]
    rows_ref[...] = jnp.zeros((32, 128), F32)
    spans = (
        (input_gain, 0, 5),
        (gain_b_ref[0:1, :], 5, 5),
        (gain_b_ref[1:2, :], 10, 5),
        (gain_f_ref[...], 15, 5),
        (gain_q_ref[...], 20, 2),
        (key_gain, 22, 2),
    )
    for vector, start, count in spans:
        for j in range(count):
            rows_ref[start + j : start + j + 1, :] = vector[:, 128 * j : 128 * j + 128]
    blocks = rows_ref[...].astype(BF16).reshape(2, 16, 128)
    for c in range(2):
        for f in range(8):
            split_ref[c, f, 30:32] = blocks
    own_ref[...] = split_ref[core]
    other_ref[...] = split_ref[1 - core]


def unpack_kernel(
    sc_ref, mine_ref, theirs_ref,
    gq_ref, gk_ref, gv_ref, gout_ref, ggate_ref, gup_ref, gdown_ref, gains_ref, both_ref,
):
    core = sc_ref[0]
    both_ref[core] = mine_ref[...]
    both_ref[1 - core] = theirs_ref[...]

    def block(c, kind, at):
        base, per = {"down": (0, 5), "wide": (80, 13), "early": (288, 4)}[kind]
        start = base + 16 * (at % per)
        return both_ref[c, at // per, start : start + 16, :].astype(F32)

    for c in range(2):
        for i in range(5):
            rows = slice(16 * i, 16 * i + 16)
            for j in range(8):
                cols = slice(256 * j + 128 * c, 256 * j + 128 * c + 128)
                ggate_ref[rows, cols] = block(c, "wide", 8 * i + j)
                gup_ref[rows, cols] = block(c, "wide", 40 + 8 * i + j)
            for j in range(4):
                gq_ref[rows, 512 * c + 128 * j : 512 * c + 128 * j + 128] = block(c, "early", 6 * i + j)
            for j in range(2):
                (gk_ref, gv_ref)[c][rows, 128 * j : 128 * j + 128] = block(c, "early", 6 * i + 4 + j)
        for i in range(8):
            for j in range(5):
                cols = slice(128 * j, 128 * j + 128)
                gdown_ref[128 * c + 16 * i : 128 * c + 16 * i + 16, cols] = block(c, "down", 5 * i + j)
                if i < 4:
                    gout_ref[64 * c + 16 * i : 64 * c + 16 * i + 16, cols] = block(
                        c, "wide", 80 + 5 * i + j
                    )
    rows = jnp.concatenate([block(0, "early", 30), block(0, "early", 31)], axis=0)
    member = sc_ref[2]
    for i, (start, count, size) in enumerate(
        ((0, 5, 80), (5, 5, 80), (10, 5, 80), (15, 5, 80), (20, 2, 32), (22, 2, 32))
    ):
        line = jnp.concatenate([rows[start + j : start + j + 1, :] for j in range(count)], axis=1)
        line = jnp.broadcast_to(line, (8, 128 * count))
        turned = pltpu.roll(line, lax.rem(128 * count - member * size, 128 * count), 1)
        gains_ref[i : i + 1, :] = turned[0:1, 0:128]


def on_device(
    tokens,
    positions,
    cotangent,
    query_weight,
    key_weight,
    value_weight,
    output_weight,
    gate_weight,
    upward_weight,
    down_weight,
    gain_input,
    gain_mixed,
    gain_hidden,
    gain_final,
    gain_query,
    gain_key,
):
    core = lax.axis_index("core")
    member = lax.axis_index(FSDP)
    scalars = jnp.stack([core, lax.axis_index("zl"), member]).astype(jnp.int32)

    gain_rows = jnp.concatenate(
        [
            jnp.pad(gain, (0, 128 - gain.shape[0]))[None, :]
            for gain in (gain_input, gain_mixed, gain_hidden, gain_final, gain_query, gain_key)
        ]
        + [jnp.zeros((2, 128), BF16)]
    ).astype(F32)
    early_spread = call(
        early_kernel,
        (scalars, query_weight, key_weight, value_weight, gain_rows),
        [SMEM] + [VMEM] * 4,
        [shape((4, 96, 768), BF16)],
    )[0]
    tall_spread, gate_spread, up_spread = call(
        late_kernel,
        (scalars, output_weight, down_weight, gate_weight, upward_weight),
        [SMEM] + [VMEM] * 4,
        [shape((4, 192, 640), BF16), shape((4, 80, 1024), BF16), shape((4, 80, 1024), BF16)],
    )
    prev = passed_along(tokens, 1)
    early_near = along_y(early_spread)
    early_parts = gathered(early_near, 3)
    tall_near = along_y(after(tall_spread, (early_near, prev)))
    tall_parts = gathered(tall_near, 1)
    gate_near = along_y(after(gate_spread, (tall_near,) + early_parts))
    gate_parts = gathered(gate_near, 3)

    before = positions[0] - ROWS + jnp.arange(ROWS, dtype=jnp.int32)
    freqs = THETA ** (-(jnp.arange(HEAD // 2, dtype=F32) * 2.0) / HEAD)
    phase = jnp.concatenate([before, positions]).astype(F32)[:, None] * freqs[None, :]
    cosine, sine = jnp.cos(phase), jnp.sin(phase)

    queries, keys, values, raw, probs, mixed, gains, mats = call(
        attend_kernel,
        (scalars, tokens, prev, cosine, sine, positions[:, None]) + early_parts,
        [SMEM] + [VMEM] * 5 + [ANY] * 4,
        [
            shape((512, 1024), BF16),
            shape((1024, 256), BF16),
            shape((1024, 256), BF16),
            shape((512, 1280), F32),
            shape((4, 2, 256, 768), BF16),
            shape((512, 1024), BF16),
            shape((16, 768), F32),
            shape((2, 8, 96, 768), BF16),
        ],
        [pltpu.SemaphoreType.DMA((4,))],
        flops=5 * 10**9,
    )
    up_near = along_y(after(up_spread, gate_near))
    up_parts = gathered(after(up_near, mixed), 1)
    wide_parts = gate_parts + up_parts
    weights_scratch = [
        pltpu.VMEM((2, 2, 8, 80, 1024), BF16),
        pltpu.VMEM((8, 2, 64, 640), BF16),
        pltpu.VMEM((2, 8, 128, 640), BF16),
    ]
    weights_sems = [pltpu.SemaphoreType.DMA((8,)), pltpu.SemaphoreType.DMA((8,))]
    layer_out, branch, middle, normed_mid, active, slope, grad_down, down_own, down_other, gain_f = call(
        forward_kernel,
        (scalars, mixed, tokens, cotangent, gains) + wide_parts + tall_parts,
        [SMEM] + [VMEM] * 4 + [ANY] * 12,
        [
            shape((512, 640), F32),
            shape((512, 640), F32),
            shape((512, 640), F32),
            shape((512, 640), BF16),
            shape((2, 512, 1024), BF16),
            shape((2, 512, 1024), BF16),
            shape((512, 640), BF16),
            shape((8, 8, 5, 16, 128), BF16),
            shape((8, 8, 5, 16, 128), BF16),
            shape((1, 640), F32),
        ],
        weights_scratch + [pltpu.VMEM((2, 512, 1024), BF16)] + weights_sems,
        flops=7 * 10**9,
    )
    down_sum = pair_sum(down_own.reshape(64, 80, 128), down_other.reshape(64, 80, 128))
    down_part = chips_sum(down_sum)
    grad_down = after(grad_down, down_sum)
    grad_middle, grad_mixed, wide_own, wide_other, gain_b = call(
        backward_kernel,
        (scalars, mixed, cotangent, gains, branch, middle, normed_mid, active, slope, grad_down)
        + wide_parts
        + tall_parts,
        [SMEM] + [VMEM] * 9 + [ANY] * 12,
        [
            shape((512, 640), F32),
            shape((512, 1024), BF16),
            shape((8, 13, 8, 16, 128), BF16),
            shape((8, 13, 8, 16, 128), BF16),
            shape((2, 640), F32),
        ],
        weights_scratch
        + [
            pltpu.VMEM((2, 512, 1024), BF16),
            pltpu.VMEM((2, 512, 1024), BF16),
            pltpu.VMEM((512, 640), BF16),
            pltpu.VMEM((2, 8, 4, 16, 640), BF16),
        ]
        + weights_sems,
        flops=8 * 10**9,
    )
    wide_other = after(wide_other, down_part)
    grad_queries, far_k, far_v, own_k, own_v = call(
        attend_back_kernel,
        (queries, keys, values, probs, grad_mixed),
        [VMEM] * 5,
        [
            shape((512, 1024), F32),
            shape((512, 256), BF16),
            shape((512, 256), BF16),
            shape((512, 256), F32),
            shape((512, 256), F32),
        ],
        [pltpu.VMEM((1024, 256), F32), pltpu.VMEM((1024, 256), F32)],
        flops=4 * 10**9,
    )
    wide_other = after(wide_other, far_k)
    back_k = passed_along(far_k, -1)
    back_v = passed_along(far_v, -1)
    wide_sum = pair_sum(wide_own.reshape(64, 208, 128), wide_other.reshape(64, 208, 128))
    wide_part = chips_sum(after(wide_sum, (back_k, back_v)))
    low_query, grad_normed, gain_q = call(
        query_back_kernel,
        (grad_queries, raw, cosine, sine, gains, mats),
        [VMEM] * 6,
        [shape((512, 1024), BF16), shape((512, 640), F32), shape((1, 256), F32)],
        flops=10**9,
    )
    grad_tokens, early_own, early_other = call(
        final_back_kernel,
        (
            scalars, tokens, low_query, grad_normed, own_k, own_v, back_k, back_v, raw, cosine, sine,
            gains, mats, grad_middle, gain_q, gain_b, gain_f,
        ),
        [SMEM] + [VMEM] * 16,
        [
            shape((512, 640), F32),
            shape((8, 32, 16, 128), BF16),
            shape((8, 32, 16, 128), BF16),
        ],
        [pltpu.VMEM((2, 8, 32, 16, 128), BF16), pltpu.VMEM((32, 128), F32)],
        flops=2 * 10**9,
    )
    early_sum = pair_sum(early_own.reshape(64, 64, 128), early_other.reshape(64, 64, 128))
    early_part = chips_sum(after(early_sum, wide_part))
    part = jnp.concatenate([down_part, wide_part, early_part], axis=0)
    mine_all = lax.all_to_all(
        jnp.broadcast_to(part[None], (8, 352, 128)), ("x", "zh"), 0, 0, tiled=True
    )
    theirs_all = swapped(mine_all)
    grads = call(
        unpack_kernel,
        (scalars, mine_all, theirs_all),
        [SMEM, VMEM, VMEM],
        [
            shape((80, 1024), F32),
            shape((80, 256), F32),
            shape((80, 256), F32),
            shape((128, 640), F32),
            shape((80, 2048), F32),
            shape((80, 2048), F32),
            shape((256, 640), F32),
            shape((8, 128), F32),
        ],
        [pltpu.VMEM((2, 8, 352, 128), BF16)],
    )
    gain_grads = [
        grads[7][i, : gain.shape[0]]
        for i, gain in enumerate((gain_input, gain_mixed, gain_hidden, gain_final, gain_query, gain_key))
    ]
    return (layer_out, grad_tokens, *grads[:7], *gain_grads)


def solution(mesh):
    fine = Mesh(mesh.devices.reshape(4, 2, 2, 2, 4), REP + FSDP)
    rows = P(REP + FSDP, None)
    weight = P(FSDP, None)
    gain = P(FSDP)
    in_specs = (rows, P(REP + FSDP), rows) + (weight,) * 7 + (gain,) * 6
    out_specs = (rows, rows) + (weight,) * 7 + (gain,) * 6
    return jax.shard_map(
        on_device, mesh=fine, in_specs=in_specs, out_specs=out_specs, check_vma=False
    )
```

```python
import jax
import jax.numpy as jnp
from jax import lax
from jax.experimental import pallas as pl
from jax.experimental.pallas import tpu as pltpu
from jax.sharding import Mesh
from jax.sharding import PartitionSpec as P

HEADS = 4
HEAD = 256
WINDOW = 512
ROWS = 512
EPS = 1e-06
THETA = 10000.0
SCALE = 0.0625
NEG = -1e30
GELU_A = 0.7978845608028654
GELU_B = 0.044715

REP = ("x", "zh", "core")
FSDP = ("zl", "y")
BF16 = jnp.bfloat16
F32 = jnp.float32
ANY = pl.BlockSpec(memory_space=pl.ANY)
VMEM = pl.BlockSpec(memory_space=pltpu.VMEM)
SMEM = pl.BlockSpec(memory_space=pltpu.SMEM)


def shape(dims, dtype):
    return jax.ShapeDtypeStruct(dims, dtype)


def call(kernel, ins, in_specs, outs, scratch=(), room=60, us=2):
    return pl.pallas_call(
        kernel,
        out_shape=outs,
        in_specs=in_specs,
        out_specs=[VMEM] * len(outs),
        scratch_shapes=list(scratch),
        compiler_params=pltpu.CompilerParams(vmem_limit_bytes=room * 1024 * 1024),
        cost_estimate=pl.CostEstimate(
            flops=us * 1_150_000_000, bytes_accessed=1, transcendentals=0
        ),
    )(*ins)


def passed_along(value, steps):
    initial, last = (max(0, -steps), min(8, 8 - steps))
    pairs = [(source, source + steps) for source in range(initial, last)]
    return lax.ppermute(value, FSDP, pairs)


def swapped(value):
    return lax.ppermute(value, "core", [(0, 1), (1, 0)])


def along_y(spread):
    return lax.all_to_all(spread, "y", 0, 0, tiled=True)


def along_z(value, steps):
    return lax.ppermute(value, ("zh", "zl"), [(i, (i + steps) % 4) for i in range(4)])


def pair_spread(near, far):
    return jnp.broadcast_to(jnp.stack([near, far])[None], (4, 2) + near.shape)


def after(value, earlier):
    return lax.optimization_barrier((value, earlier))[0]


def chips_sum(both):
    parts = lax.all_to_all(both, ("zl", "y", "x", "zh"), 0, 0, tiled=True)
    return jnp.sum(parts.astype(F32), axis=0).astype(BF16)


def normalize(values):
    factor = lax.rsqrt(jnp.mean(values * values, axis=-1, keepdims=True) + EPS)
    return (values * factor, factor)


def norm_back(grad_hat, unit, factor):
    return factor * (grad_hat - unit * jnp.mean(grad_hat * unit, axis=-1, keepdims=True))


def rotate(values, cosine, sine):
    first, second = values[:, :128], values[:, 128:]
    return jnp.concatenate(
        [first * cosine - second * sine, second * cosine + first * sine], axis=-1
    )


def product(left, right):
    return jnp.dot(left, right, preferred_element_type=F32)


def product_rt(left, right):
    return lax.dot_general(left, right, (((1,), (1,)), ((), ())), preferred_element_type=F32)


def product_lt(left, right):
    return lax.dot_general(left, right, (((0,), (0,)), ((), ())), preferred_element_type=F32)


def column_sum(values):
    return jnp.sum(values, axis=0, keepdims=True)


def load_early(pieces, target, core, zl, sems):
    copies = []
    for i, piece in enumerate(pieces):
        half = core if i < 2 else 1 - core
        group = zl if i % 2 == 0 else 1 - zl
        place = target.at[half, pl.ds(group * 4, 4)]
        parts = [(piece.at[:, 0:80], place.at[:, 0:80, 0:640]), (piece.at[:, 96:112], place.at[:, 80:96, 0:640])]
        for k in range(5):
            rows = slice(16 * k, 16 * k + 16)
            parts.append((piece.at[:, 80:96, 128 * k : 128 * k + 128], place.at[:, rows, 640:768]))
        for k, (source, where) in enumerate(parts):
            copies.append(pltpu.make_async_copy(source, where, sems.at[7 * i + k]))
    for copy in copies:
        copy.start()
    return copies


def early_kernel(sc_ref, query_ref, key_ref, value_ref, output_ref, down_ref, gains_ref, out_ref):
    core, member = sc_ref[0], sc_ref[2]
    for c, last in enumerate((key_ref, value_ref)):

        @pl.when(core == c)
        def _():
            for k in range(4):
                out_ref[k, 0:80, 0:512] = query_ref[:, 512 * c : 512 * c + 512]
                out_ref[k, 0:80, 512:640] = last[:, 0:128]
                for i in range(5):
                    out_ref[k, 80:96, 128 * i : 128 * i + 128] = last[16 * i : 16 * i + 16, 128:256]
                out_ref[k, 112:176, :] = output_ref[64 * c : 64 * c + 64, :]
                out_ref[k, 176:304, :] = down_ref[128 * c : 128 * c + 128, :]

    padded = jnp.concatenate([gains_ref[...], jnp.zeros((8, 512), F32)], axis=1)
    model = pltpu.roll(padded, member * 80, 1)
    head = pltpu.roll(padded, member * 32, 1)
    which = lax.broadcasted_iota(jnp.int32, (8, 640), 0)
    rows = jnp.concatenate([jnp.where(which < 4, model, head), jnp.zeros((8, 640), F32)], axis=0)
    for k in range(4):
        out_ref[k, 96:112, :] = rows.astype(BF16)


def late_kernel(sc_ref, gate_ref, up_ref, wide_out):
    core = sc_ref[0]
    for c in range(2):

        @pl.when(core == c)
        def _():
            for f in range(8):
                cols = slice(128 * f, 128 * f + 128)
                source = slice(256 * f + 128 * c, 256 * f + 128 * c + 128)
                wide_out[0, :, cols] = gate_ref[:, source]
                wide_out[1, :, cols] = up_ref[:, source]


def attend_kernel(
    sc_ref, tok_ref, prev_ref, cos_ref, sin_ref, pos_ref, near, far, near_t, far_t,
    q_ref, k_ref, v_ref, raw_ref, p_ref, mixed_ref, gains_ref, normed_ref, e_ref, sems,
):
    core, zl = sc_ref[0], sc_ref[1]
    copies = load_early((near, far, near_t, far_t), e_ref, core, zl, sems)
    unit, _ = normalize(tok_ref[...].astype(F32))
    unit_prev, _ = normalize(prev_ref[...].astype(F32))
    for copy in copies:
        copy.wait()
    gains = jnp.sum(e_ref[0, :, 80:96, 0:640].astype(F32), axis=0)
    gains_ref[...] = gains
    normed = (unit * gains[0:1, :640]).astype(BF16)
    normed_ref[...] = normed
    normed_prev = (unit_prev * gains[0:1, :640]).astype(BF16)
    g_query, g_key = gains[4:5, :256], gains[5:6, :256]
    mat_0 = e_ref[0, :, 0:80, :].reshape(640, 768)
    mat_1 = e_ref[1, :, 0:80, :].reshape(640, 768)
    raw_0 = product(normed, mat_0)
    raw_1 = product(normed, mat_1)
    raw_ref[:, 0:512] = raw_0[:, :512]
    raw_ref[:, 512:1024] = raw_1[:, :512]
    raw_ref[:, 1024:1280] = raw_0[:, 512:]
    v_ref[0:512, :] = product(normed_prev, mat_1[:, 512:]).astype(BF16)
    v_ref[512:1024, :] = raw_1[:, 512:].astype(BF16)
    prev_unit, _ = normalize(product(normed_prev, mat_0[:, 512:]))
    k_ref[0:512, :] = rotate(prev_unit * g_key, cos_ref[0:512, :], sin_ref[0:512, :]).astype(BF16)
    cosine, sine = cos_ref[512:1024, :], sin_ref[512:1024, :]
    own_unit, _ = normalize(raw_0[:, 512:])
    k_ref[512:1024, :] = rotate(own_unit * g_key, cosine, sine).astype(BF16)
    for h in range(HEADS):
        q_unit, _ = normalize(raw_ref[:, 256 * h : 256 * h + 256])
        turned = rotate(q_unit * g_query, cosine, sine).astype(BF16)
        q_ref[:, 256 * h : 256 * h + 256] = turned * BF16(SCALE)
    for b in range(2):
        rows = slice(256 * b, 256 * b + 256)
        keys = slice(256 * b, 256 * b + 768)
        query_at = lax.broadcasted_iota(jnp.int32, (256, 768), 0)
        key_at = lax.broadcasted_iota(jnp.int32, (256, 768), 1) - 512
        back = query_at - key_at
        allowed = (back >= 0) & (back < WINDOW) & (back <= pos_ref[rows, :])
        for h in range(HEADS):
            cols = slice(256 * h, 256 * h + 256)
            scores = jnp.where(allowed, product_rt(q_ref[rows, cols], k_ref[keys, :]), NEG)
            expd = jnp.exp(scores - jnp.max(scores, axis=-1, keepdims=True))
            probs = (expd / jnp.sum(expd, axis=-1, keepdims=True)).astype(BF16)
            p_ref[h, b] = probs
            mixed_ref[rows, cols] = product(probs, v_ref[keys, :]).astype(BF16)


def load_wide(pieces, target, zl, sems):
    copies = []
    for half, piece in enumerate(pieces):
        for near in range(2):
            group = zl if near == 0 else 1 - zl
            for k in range(2):
                place = target.at[k, half, pl.ds(group * 4, 4)]
                sem = sems.at[4 * half + 2 * near + k]
                copies.append(pltpu.make_async_copy(piece.at[:, near, k], place, sem))
    for copy in copies:
        copy.start()
    return copies


def load_out(pieces, out_w, core, zl, sems):
    copies = []
    for i, piece in enumerate(pieces):
        half = core if i < 2 else 1 - core
        group = zl if i % 2 == 0 else 1 - zl
        place = out_w.at[pl.ds(group * 4, 4), half]
        copies.append(pltpu.make_async_copy(piece.at[:, 0:64], place, sems.at[i]))
    for copy in copies:
        copy.start()
    return copies


def load_down(pieces, down_w, zl, sems):
    copies = []
    for i, piece in enumerate(pieces):
        group = zl if i % 2 == 0 else 1 - zl
        place = down_w.at[i // 2, pl.ds(group * 4, 4)]
        copies.append(pltpu.make_async_copy(piece.at[:, 64:192], place, sems.at[i]))
    for copy in copies:
        copy.start()
    return copies


def forward_kernel(
    sc_ref, mixed_ref, tok_ref, cot_ref, gains_ref, w0, w1, t0, t1, t2, t3,
    out_ref, branch_ref, middle_ref, nm_ref, act_ref, slope_ref, gd_ref, hid_own_ref, other_ref, gain_ref,
    wide_w, out_w, down_w, hid_other_ref, wide_sems, out_sems, down_sems,
):
    core, zl = sc_ref[0], sc_ref[1]
    tall = load_out((t0, t1, t2, t3), out_w, core, zl, out_sems)
    wide = load_wide((w0, w1), wide_w, zl, wide_sems)
    wide += load_down((t0, t1, t2, t3), down_w, zl, down_sems)
    hid_refs = (hid_own_ref, hid_other_ref)
    for copy in tall:
        copy.wait()
    g_mixed, g_hidden, g_final = [gains_ref[i : i + 1, :640] for i in (1, 2, 3)]
    out_mat = out_w[...].reshape(1024, 640)
    branch_ref[...] = product(mixed_ref[...], out_mat)
    for copy in wide:
        copy.wait()
    gain_sum = jnp.zeros((1, 640), F32)
    for b in range(2):
        rows = slice(256 * b, 256 * b + 256)
        branch_unit, _ = normalize(branch_ref[rows, :])
        middle = tok_ref[rows, :].astype(F32) + branch_unit * g_mixed
        middle_ref[rows, :] = middle
        mid_unit, _ = normalize(middle)
        normed = (mid_unit * g_hidden).astype(BF16)
        nm_ref[rows, :] = normed
        down = jnp.zeros((256, 640), F32)
        for half in range(2):
            for n in range(2):
                cols = slice(512 * n, 512 * n + 512)
                u = product(normed, wide_w[0, half, :, :, cols].reshape(640, 512))
                upward = product(normed, wide_w[1, half, :, :, cols].reshape(640, 512))
                square = u * u
                t = jnp.tanh(GELU_A * u * (1.0 + GELU_B * square))
                side = 0.5 * (1.0 + t)
                active = u * side
                slope = side + 0.5 * u * (1.0 - t * t) * (GELU_A * (1.0 + 3.0 * GELU_B * square))
                act_ref[half, rows, cols] = active.astype(BF16)
                slope_ref[half, rows, cols] = (slope * upward).astype(BF16)
                hidden = (active * upward).astype(BF16)
                hid_refs[half][rows, cols] = hidden
                mat = down_w[half, 4 * n : 4 * n + 4].reshape(512, 640)
                down = down + product(hidden, mat)
        down_unit, down_factor = normalize(down)
        out_ref[rows, :] = middle + down_unit * g_final
        grad_out = cot_ref[rows, :].astype(F32)
        gain_sum = gain_sum + column_sum(grad_out * down_unit)
        gd_ref[rows, :] = norm_back(grad_out * g_final, down_unit, down_factor).astype(BF16)
    gain_ref[...] = gain_sum
    down_blocks(hid_other_ref, gd_ref, None, other_ref)


def down_blocks(hid_ref, gd_ref, received, ref):
    for n in range(2):
        members = slice(4 * n, 4 * n + 4)
        part = product_lt(hid_ref[:, 512 * n : 512 * n + 512], gd_ref[...]).reshape(4, 8, 16, 640)
        for j in range(5):
            block = part[:, :, :, 128 * j : 128 * j + 128]
            if received is not None:
                block = block + received[members, :, j].astype(F32)
            ref[members, :, j] = block.astype(BF16)


def down_own_kernel(hid_ref, gd_ref, received, ref):
    down_blocks(hid_ref, gd_ref, received, ref)


def wide_blocks(nm_ref, grads, received, ref):
    for at, grad_ref in enumerate(grads):
        for n in range(2):
            part = product_lt(nm_ref[...], grad_ref[:, 512 * n : 512 * n + 512])
            part = part.reshape(8, 5, 16, 512)
            for j in range(4):
                block = part[:, :, :, 128 * j : 128 * j + 128]
                if received is not None:
                    block = block + received[:, 5 * at : 5 * at + 5, 4 * n + j].astype(F32)
                ref[:, 5 * at : 5 * at + 5, 4 * n + j] = block.astype(BF16)


def backward_kernel(
    sc_ref, act_ref, slope_ref, gd_ref, nm_ref, mixed_ref, cot_ref, gains_ref, branch_ref, middle_ref,
    w0, w1, t0, t1, t2, t3,
    gg_own_ref, gu_own_ref, wide_other_ref, gmid_ref, gmixed_ref, own_ref, other_ref, gain_ref,
    gg_other_ref, gu_other_ref, wide_w, out_w, down_w, gb_ref, split_ref, wide_sems, out_sems, down_sems,
):
    core, zl = sc_ref[0], sc_ref[1]
    down = load_down((t0, t1, t2, t3), down_w, sc_ref[1], down_sems)
    wide = load_wide((w0, w1), wide_w, zl, wide_sems)
    wide += load_out((t0, t1, t2, t3), out_w, core, zl, out_sems)
    for copy in down:
        copy.wait()
    for half, (gg_ref, gu_ref) in enumerate(((gg_own_ref, gu_own_ref), (gg_other_ref, gu_other_ref))):
        for n in range(2):
            cols = slice(512 * n, 512 * n + 512)
            mat = down_w[half, 4 * n : 4 * n + 4].reshape(512, 640)
            grad_hidden = product_rt(gd_ref[...], mat)
            gg_ref[:, cols] = (grad_hidden * slope_ref[half, :, cols].astype(F32)).astype(BF16)
            gu_ref[:, cols] = (grad_hidden * act_ref[half, :, cols].astype(F32)).astype(BF16)
    wide_blocks(nm_ref, (gg_other_ref, gu_other_ref), None, wide_other_ref)
    for copy in wide:
        copy.wait()
    g_mixed, g_hidden = [gains_ref[i : i + 1, :640] for i in (1, 2)]
    sum_mixed = jnp.zeros((1, 640), F32)
    sum_hidden = jnp.zeros((1, 640), F32)
    for b in range(2):
        rows = slice(256 * b, 256 * b + 256)
        grad_normed = jnp.zeros((256, 640), F32)
        for half, refs in enumerate(((gg_own_ref, gu_own_ref), (gg_other_ref, gu_other_ref))):
            for at, ref in enumerate(refs):
                grad_normed = grad_normed + product_rt(
                    ref[rows, :], wide_w[at, half].reshape(640, 1024)
                )
        mid_unit, mid_factor = normalize(middle_ref[rows, :])
        sum_hidden = sum_hidden + column_sum(grad_normed * mid_unit)
        grad_middle = cot_ref[rows, :].astype(F32) + norm_back(
            grad_normed * g_hidden, mid_unit, mid_factor
        )
        gmid_ref[rows, :] = grad_middle
        branch_unit, branch_factor = normalize(branch_ref[rows, :])
        sum_mixed = sum_mixed + column_sum(grad_middle * branch_unit)
        grad_branch = norm_back(grad_middle * g_mixed, branch_unit, branch_factor).astype(BF16)
        gb_ref[rows, :] = grad_branch
        gmixed_ref[rows, :] = product_rt(grad_branch, out_w[...].reshape(1024, 640)).astype(BF16)
    gain_ref[0:1, :] = sum_mixed
    gain_ref[1:2, :] = sum_hidden
    for n in range(2):
        part = product_lt(mixed_ref[:, 512 * n : 512 * n + 512], gb_ref[...])
        part = part.astype(BF16).reshape(4, 2, 4, 16, 640)
        for c in range(2):
            split_ref[c, 4 * n : 4 * n + 4] = part[:, c]
    for half, ref in ((core, own_ref), (1 - core, other_ref)):
        part = split_ref[half]
        for i in range(4):
            for j in range(5):
                ref[:, i * 5 + j] = part[:, i, :, 128 * j : 128 * j + 128]


def wide_own_kernel(nm_ref, gg_ref, gu_ref, received, out_own, out_received, ref):
    wide_blocks(nm_ref, (gg_ref, gu_ref), received, ref)
    for at in range(20):
        block = out_own[:, at].astype(F32) + out_received[:, at].astype(F32)
        ref[:, 10 + at // 8, at % 8] = block.astype(BF16)
    ref[:, 12, 4:8] = jnp.zeros((8, 4, 16, 128), BF16)


def attend_back_kernel(
    q_ref, k_ref, v_ref, p_ref, gm_ref, gq_ref, far_k_ref, far_v_ref, own_k_ref, own_v_ref, dk_ref, dv_ref
):
    dk_ref[...] = jnp.zeros((1024, 256), F32)
    dv_ref[...] = jnp.zeros((1024, 256), F32)
    for b in range(2):
        rows = slice(256 * b, 256 * b + 256)
        keys = slice(256 * b, 256 * b + 768)
        for h in range(HEADS):
            cols = slice(256 * h, 256 * h + 256)
            probs = p_ref[h, b]
            grads = gm_ref[rows, cols]
            weighed = probs.astype(F32)
            grad_probs = product_rt(grads, v_ref[keys, :])
            inner = jnp.sum(weighed * grad_probs, axis=-1, keepdims=True)
            grad_scores = (weighed * (grad_probs - inner)).astype(BF16)
            gq_ref[rows, cols] = product(grad_scores, k_ref[keys, :]) * SCALE
            dk_ref[keys, :] += product_lt(grad_scores, q_ref[rows, cols])
            dv_ref[keys, :] += product_lt(probs, grads)
    far_k_ref[...] = dk_ref[0:512, :].astype(BF16)
    far_v_ref[...] = dv_ref[0:512, :].astype(BF16)
    own_k_ref[...] = dk_ref[512:1024, :]
    own_v_ref[...] = dv_ref[512:1024, :]


def query_back_kernel(gq_ref, raw_ref, cos_ref, sin_ref, gains_ref, e_ref, low_ref, gn_ref, gain_ref):
    cosine, sine = cos_ref[512:1024, :], sin_ref[512:1024, :]
    g_query = gains_ref[4:5, :256]
    total = jnp.zeros((1, 256), F32)
    for h in range(HEADS):
        cols = slice(256 * h, 256 * h + 256)
        turned = rotate(gq_ref[:, cols], cosine, -sine)
        unit, factor = normalize(raw_ref[:, cols])
        total = total + column_sum(turned * unit)
        low_ref[:, cols] = norm_back(turned * g_query, unit, factor).astype(BF16)
    gain_ref[...] = total
    gn_ref[...] = product_rt(
        low_ref[:, 0:512], e_ref[0, :, 0:80, 0:512].reshape(640, 512)
    ) + product_rt(low_ref[:, 512:1024], e_ref[1, :, 0:80, 0:512].reshape(640, 512))


def early_blocks(heads, last, normed_ref, received, ref):
    for grads, at in ((heads, 0), (last, 4)):
        part = product_lt(normed_ref[...], grads).reshape(8, 5, 16, grads.shape[1])
        for i in range(5):
            for j in range(grads.shape[1] // 128):
                block = part[:, i, :, 128 * j : 128 * j + 128]
                if received is not None:
                    block = block + received[:, i * 6 + at + j].astype(F32)
                ref[:, i * 6 + at + j] = block.astype(BF16)


def key_back_kernel(
    sc_ref, normed_ref, low_ref, own_k_ref, own_v_ref, back_k_ref, back_v_ref, raw_ref, cos_ref, sin_ref,
    gains_ref, gk_ref, gv_ref, other_ref, gain_ref,
):
    other = 1 - sc_ref[0]
    cosine, sine = cos_ref[512:1024, :], sin_ref[512:1024, :]
    key_grad = own_k_ref[...] + back_k_ref[...].astype(F32)
    gv_ref[...] = (own_v_ref[...] + back_v_ref[...].astype(F32)).astype(BF16)
    turned = rotate(key_grad, cosine, -sine)
    unit, factor = normalize(raw_ref[:, 1024:1280])
    gain_ref[...] = column_sum(turned * unit)
    gk_ref[...] = norm_back(turned * gains_ref[5:6, :256], unit, factor).astype(BF16)
    last = jnp.where(other == 0, gk_ref[...].astype(F32), gv_ref[...].astype(F32)).astype(BF16)
    heads = low_ref[:, pl.ds(pl.multiple_of(other * 512, 512), 512)]
    early_blocks(heads, last, normed_ref, None, other_ref)


def token_back_kernel(
    tok_ref, gn_ref, gk_ref, gv_ref, gains_ref, e_ref, gmid_ref, gtok_ref, gain_ref
):
    grad_normed = (
        gn_ref[...]
        + product_rt(gk_ref[...], e_ref[0, :, 0:80, 512:768].reshape(640, 256))
        + product_rt(gv_ref[...], e_ref[1, :, 0:80, 512:768].reshape(640, 256))
    )
    unit_in, factor_in = normalize(tok_ref[...].astype(F32))
    gain_ref[...] = column_sum(grad_normed * unit_in)
    gtok_ref[...] = gmid_ref[...] + norm_back(grad_normed * gains_ref[0:1, :640], unit_in, factor_in)


def early_own_kernel(
    sc_ref, normed_ref, low_ref, gk_ref, gv_ref, received, gain_i_ref, gain_b_ref, gain_f_ref, gain_q_ref,
    gain_k_ref, ref, rows_ref,
):
    core = sc_ref[0]
    last = jnp.where(core == 0, gk_ref[...].astype(F32), gv_ref[...].astype(F32)).astype(BF16)
    heads = low_ref[:, pl.ds(pl.multiple_of(core * 512, 512), 512)]
    early_blocks(heads, last, normed_ref, received, ref)
    rows_ref[...] = jnp.zeros((32, 128), F32)
    spans = (
        (gain_i_ref[...], 0, 5),
        (gain_b_ref[0:1, :], 5, 5),
        (gain_b_ref[1:2, :], 10, 5),
        (gain_f_ref[...], 15, 5),
        (gain_q_ref[...], 20, 2),
        (gain_k_ref[...], 22, 2),
    )
    for vector, start, count in spans:
        for j in range(count):
            rows_ref[start + j : start + j + 1, :] = vector[:, 128 * j : 128 * j + 128]
    blocks = rows_ref[...].astype(BF16).reshape(2, 16, 128)
    for f in range(8):
        ref[f, 30:32] = blocks


def unpack_kernel(
    sc_ref, mine_ref, theirs_ref,
    gq_ref, gk_ref, gv_ref, gout_ref, ggate_ref, gup_ref, gdown_ref,
    gain_0, gain_1, gain_2, gain_3, gain_4, gain_5, both_ref,
):
    core = sc_ref[0]
    both_ref[core] = mine_ref[...]
    both_ref[1 - core] = theirs_ref[...]

    def block(c, kind, at):
        base, per = {"down": (0, 5), "wide": (80, 13), "early": (288, 4)}[kind]
        start = base + 16 * (at % per)
        return both_ref[c, at // per, start : start + 16, :].astype(F32)

    for c in range(2):
        for i in range(5):
            rows = slice(16 * i, 16 * i + 16)
            for j in range(8):
                cols = slice(256 * j + 128 * c, 256 * j + 128 * c + 128)
                ggate_ref[rows, cols] = block(c, "wide", 8 * i + j)
                gup_ref[rows, cols] = block(c, "wide", 40 + 8 * i + j)
            for j in range(4):
                gq_ref[rows, 512 * c + 128 * j : 512 * c + 128 * j + 128] = block(c, "early", 6 * i + j)
            for j in range(2):
                (gk_ref, gv_ref)[c][rows, 128 * j : 128 * j + 128] = block(c, "early", 6 * i + 4 + j)
        for i in range(8):
            for j in range(5):
                cols = slice(128 * j, 128 * j + 128)
                gdown_ref[128 * c + 16 * i : 128 * c + 16 * i + 16, cols] = block(c, "down", 5 * i + j)
                if i < 4:
                    gout_ref[64 * c + 16 * i : 64 * c + 16 * i + 16, cols] = block(
                        c, "wide", 80 + 5 * i + j
                    )
    rows = jnp.concatenate(
        [block(0, "early", at) + block(1, "early", at) for at in (30, 31)], axis=0
    )
    member = sc_ref[2]
    for i, (start, count, size) in enumerate(
        ((0, 5, 80), (5, 5, 80), (10, 5, 80), (15, 5, 80), (20, 2, 32), (22, 2, 32))
    ):
        line = jnp.concatenate([rows[start + j : start + j + 1, :] for j in range(count)], axis=1)
        line = jnp.broadcast_to(line, (8, 128 * count))
        turned = pltpu.roll(line, lax.rem(128 * count - member * size, 128 * count), 1)
        (gain_0, gain_1, gain_2, gain_3, gain_4, gain_5)[i][...] = turned[0:1, 0:size]


def on_device(
    tokens,
    positions,
    cotangent,
    query_weight,
    key_weight,
    value_weight,
    output_weight,
    gate_weight,
    upward_weight,
    down_weight,
    gain_input,
    gain_mixed,
    gain_hidden,
    gain_final,
    gain_query,
    gain_key,
):
    core = lax.axis_index("core")
    member = lax.axis_index(FSDP)
    scalars = jnp.stack([core, lax.axis_index("zl"), member]).astype(jnp.int32)

    gain_rows = jnp.concatenate(
        [
            jnp.pad(gain, (0, 128 - gain.shape[0]))[None, :]
            for gain in (gain_input, gain_mixed, gain_hidden, gain_final, gain_query, gain_key)
        ]
        + [jnp.zeros((2, 128), BF16)]
    ).astype(F32)
    early_spread = call(
        early_kernel,
        (scalars, query_weight, key_weight, value_weight, output_weight, down_weight, gain_rows),
        [SMEM] + [VMEM] * 6,
        [shape((4, 304, 640), BF16)],
    )[0]
    wide = call(
        late_kernel, (scalars, gate_weight, upward_weight), [SMEM] + [VMEM] * 2, [shape((2, 80, 1024), BF16)]
    )[0]
    prev = passed_along(tokens, 1)
    wide_far = along_z(wide, 1)
    near = along_y(early_spread)
    wide_own = along_y(pair_spread(wide, after(wide_far, (near, prev))))
    early_near, tall_near = near[:, :112], near[:, 112:]
    early_far = along_z(early_near, 3)
    early_parts = (early_near, early_far, swapped(early_near), swapped(early_far))
    tall_far = along_z(tall_near, 1)
    tall_parts = (tall_near, tall_far, swapped(tall_near), swapped(tall_far))

    before = positions[0] - ROWS + jnp.arange(ROWS, dtype=jnp.int32)
    freqs = THETA ** (-(jnp.arange(HEAD // 2, dtype=F32) * 2.0) / HEAD)
    phase = jnp.concatenate([before, positions]).astype(F32)[:, None] * freqs[None, :]
    cosine, sine = jnp.cos(phase), jnp.sin(phase)

    queries, keys, values, raw, probs, mixed, gains, normed, mats = call(
        attend_kernel,
        (scalars, tokens, prev, cosine, sine, positions[:, None]) + early_parts,
        [SMEM] + [VMEM] * 5 + [ANY] * 4,
        [
            shape((512, 1024), BF16),
            shape((1024, 256), BF16),
            shape((1024, 256), BF16),
            shape((512, 1280), F32),
            shape((4, 2, 256, 768), BF16),
            shape((512, 1024), BF16),
            shape((16, 640), F32),
            shape((512, 640), BF16),
            shape((2, 8, 96, 768), BF16),
        ],
        [pltpu.SemaphoreType.DMA((28,))],
        us=9,
    )
    wide_own = after(wide_own, (mixed,) + tall_parts)
    wide_parts = (wide_own, swapped(wide_own))
    wide_scratch = pltpu.VMEM((2, 2, 8, 80, 1024), BF16)
    out_scratch = pltpu.VMEM((8, 2, 64, 640), BF16)
    down_scratch = pltpu.VMEM((2, 8, 128, 640), BF16)
    sems_4, sems_8 = pltpu.SemaphoreType.DMA((4,)), pltpu.SemaphoreType.DMA((8,))
    layer_out, branch, middle, normed_mid, active, slope, grad_down, hid_own, down_other, gain_f = call(
        forward_kernel,
        (scalars, mixed, tokens, cotangent, gains) + wide_parts + tall_parts,
        [SMEM] + [VMEM] * 4 + [ANY] * 6,
        [
            shape((512, 640), F32),
            shape((512, 640), F32),
            shape((512, 640), F32),
            shape((512, 640), BF16),
            shape((2, 512, 1024), BF16),
            shape((2, 512, 1024), BF16),
            shape((512, 640), BF16),
            shape((512, 1024), BF16),
            shape((8, 8, 5, 16, 128), BF16),
            shape((1, 640), F32),
        ],
        [wide_scratch, out_scratch, down_scratch, pltpu.VMEM((512, 1024), BF16), sems_8, sems_4, sems_4],
        us=13,
    )
    down_sum = call(
        down_own_kernel,
        (hid_own, grad_down, swapped(down_other)),
        [VMEM] * 3,
        [shape((8, 8, 5, 16, 128), BF16)],
    )[0]
    down_part = chips_sum(down_sum.reshape(64, 80, 128))
    gg_own, gu_own, wide_other, grad_middle, grad_mixed, out_own, out_other, gain_b = call(
        backward_kernel,
        (
            scalars, active, slope, after(grad_down, down_sum), normed_mid, mixed, cotangent, gains, branch,
            middle,
        )
        + wide_parts
        + tall_parts,
        [SMEM] + [VMEM] * 9 + [ANY] * 6,
        [
            shape((512, 1024), BF16),
            shape((512, 1024), BF16),
            shape((8, 10, 8, 16, 128), BF16),
            shape((512, 640), F32),
            shape((512, 1024), BF16),
            shape((8, 20, 16, 128), BF16),
            shape((8, 20, 16, 128), BF16),
            shape((2, 640), F32),
        ],
        [
            pltpu.VMEM((512, 1024), BF16),
            pltpu.VMEM((512, 1024), BF16),
            wide_scratch,
            out_scratch,
            down_scratch,
            pltpu.VMEM((512, 640), BF16),
            pltpu.VMEM((2, 8, 4, 16, 640), BF16),
            sems_8,
            sems_4,
            sems_4,
        ],
        us=17,
    )
    wide_received = swapped(after(wide_other, down_part))
    grad_queries, far_k, far_v, own_k, own_v = call(
        attend_back_kernel,
        (queries, keys, values, probs, grad_mixed),
        [VMEM] * 5,
        [
            shape((512, 1024), F32),
            shape((512, 256), BF16),
            shape((512, 256), BF16),
            shape((512, 256), F32),
            shape((512, 256), F32),
        ],
        [pltpu.VMEM((1024, 256), F32), pltpu.VMEM((1024, 256), F32)],
        us=6,
    )
    back_k = passed_along(far_k, -1)
    back_v = passed_along(far_v, -1)
    wide_sum = call(
        wide_own_kernel,
        (after(normed_mid, far_k), gg_own, gu_own, wide_received, out_own, swapped(after(out_other, down_part))),
        [VMEM] * 6,
        [shape((8, 13, 8, 16, 128), BF16)],
        us=5,
    )[0]
    wide_part = chips_sum(after(wide_sum.reshape(64, 208, 128), (down_part, back_k, back_v)))
    grad_queries = after(grad_queries, wide_sum)
    low_query, grad_normed, gain_q = call(
        query_back_kernel,
        (grad_queries, raw, cosine, sine, gains, mats),
        [VMEM] * 6,
        [shape((512, 1024), BF16), shape((512, 640), F32), shape((1, 256), F32)],
    )
    small = shape((512, 256), BF16)
    grad_key, grad_value, early_other, gain_k = call(
        key_back_kernel,
        (scalars, normed, low_query, own_k, own_v, back_k, back_v, raw, cosine, sine, gains),
        [SMEM] + [VMEM] * 10,
        [small, small, shape((8, 30, 16, 128), BF16), shape((1, 256), F32)],
    )
    early_received = swapped(early_other)
    grad_tokens, gain_i = call(
        token_back_kernel,
        (tokens, grad_normed, grad_key, grad_value, gains, mats, grad_middle),
        [VMEM] * 7,
        [shape((512, 640), F32), shape((1, 640), F32)],
    )
    early_sum = call(
        early_own_kernel,
        (
            scalars, normed, low_query, grad_key, grad_value, early_received, gain_i, gain_b, gain_f, gain_q,
            gain_k,
        ),
        [SMEM] + [VMEM] * 10,
        [shape((8, 32, 16, 128), BF16)],
        [pltpu.VMEM((32, 128), F32)],
    )[0]
    early_part = chips_sum(after(early_sum.reshape(64, 64, 128), wide_part))
    part = jnp.concatenate([down_part, wide_part, early_part], axis=0)
    mine_all = lax.all_to_all(
        jnp.broadcast_to(part[None], (8, 352, 128)), ("x", "zh"), 0, 0, tiled=True
    )
    theirs_all = swapped(mine_all)
    grads = call(
        unpack_kernel,
        (scalars, mine_all, theirs_all),
        [SMEM, VMEM, VMEM],
        [
            shape((80, 1024), F32),
            shape((80, 256), F32),
            shape((80, 256), F32),
            shape((128, 640), F32),
            shape((80, 2048), F32),
            shape((80, 2048), F32),
            shape((256, 640), F32),
            *[shape((1, size), F32) for size in (80, 80, 80, 80, 32, 32)],
        ],
        [pltpu.VMEM((2, 8, 352, 128), BF16)],
    )
    gain_grads = [grad.reshape(-1) for grad in grads[7:]]
    return (layer_out, grad_tokens, *grads[:7], *gain_grads)


def solution(mesh):
    fine = Mesh(mesh.devices.reshape(4, 2, 2, 2, 4), REP + FSDP)
    rows = P(REP + FSDP, None)
    weight = P(FSDP, None)
    gain = P(FSDP)
    in_specs = (rows, P(REP + FSDP), rows) + (weight,) * 7 + (gain,) * 6
    out_specs = (rows, rows) + (weight,) * 7 + (gain,) * 6
    return jax.shard_map(
        on_device, mesh=fine, in_specs=in_specs, out_specs=out_specs, check_vma=False
    )
```

```python
import jax
import jax.numpy as jnp
from jax import lax
from jax.experimental import pallas as pl
from jax.experimental.pallas import tpu as pltpu
from jax.sharding import Mesh
from jax.sharding import PartitionSpec as P

HEADS = 4
HEAD = 256
WINDOW = 512
ROWS = 512
EPS = 1e-06
THETA = 10000.0
SCALE = 0.0625
NEG = -1e30
GELU_A = 0.7978845608028654
GELU_B = 0.044715

REP = ("x", "zh", "core")
FSDP = ("zl", "y")
BF16 = jnp.bfloat16
F32 = jnp.float32
ANY = pl.BlockSpec(memory_space=pl.ANY)
VMEM = pl.BlockSpec(memory_space=pltpu.VMEM)
SMEM = pl.BlockSpec(memory_space=pltpu.SMEM)


def shape(dims, dtype):
    return jax.ShapeDtypeStruct(dims, dtype)


def call(kernel, ins, in_specs, outs, scratch=(), room=60, us=2):
    return pl.pallas_call(
        kernel,
        out_shape=outs,
        in_specs=in_specs,
        out_specs=[VMEM] * len(outs),
        scratch_shapes=list(scratch),
        compiler_params=pltpu.CompilerParams(vmem_limit_bytes=room * 1024 * 1024),
        cost_estimate=pl.CostEstimate(
            flops=us * 1_150_000_000, bytes_accessed=1, transcendentals=0
        ),
    )(*ins)


def passed_along(value, steps):
    initial, last = (max(0, -steps), min(8, 8 - steps))
    pairs = [(source, source + steps) for source in range(initial, last)]
    return lax.ppermute(value, FSDP, pairs)


def swapped(value):
    return lax.ppermute(value, "core", [(0, 1), (1, 0)])


def along_y(spread):
    return lax.all_to_all(spread, "y", 0, 0, tiled=True)


def along_z(value, steps):
    return lax.ppermute(value, ("zh", "zl"), [(i, (i + steps) % 4) for i in range(4)])


def pair_spread(near, far):
    return jnp.broadcast_to(jnp.stack([near, far])[None], (4, 2) + near.shape)


def after(value, earlier):
    return lax.optimization_barrier((value, earlier))[0]


def chips_sum(both):
    parts = lax.all_to_all(both, ("zl", "y", "x", "zh"), 0, 0, tiled=True)
    return jnp.sum(parts.astype(F32), axis=0).astype(BF16)


def normalize(values):
    factor = lax.rsqrt(jnp.mean(values * values, axis=-1, keepdims=True) + EPS)
    return (values * factor, factor)


def norm_back(grad_hat, unit, factor):
    return factor * (grad_hat - unit * jnp.mean(grad_hat * unit, axis=-1, keepdims=True))


def rotate(values, cosine, sine):
    first, second = values[:, :128], values[:, 128:]
    return jnp.concatenate(
        [first * cosine - second * sine, second * cosine + first * sine], axis=-1
    )


def product(left, right):
    return jnp.dot(left, right, preferred_element_type=F32)


def product_rt(left, right):
    return lax.dot_general(left, right, (((1,), (1,)), ((), ())), preferred_element_type=F32)


def product_lt(left, right):
    return lax.dot_general(left, right, (((0,), (0,)), ((), ())), preferred_element_type=F32)


def column_sum(values):
    return jnp.sum(values, axis=0, keepdims=True)


def load_early(pieces, target, core, zl, sems):
    copies = []
    for i, piece in enumerate(pieces):
        half = core if i < 2 else 1 - core
        group = zl if i % 2 == 0 else 1 - zl
        place = target.at[half, pl.ds(group * 4, 4)]
        parts = [(piece.at[:, 0:80], place.at[:, 0:80, 0:640]), (piece.at[:, 96:112], place.at[:, 80:96, 0:640])]
        for k in range(5):
            rows = slice(16 * k, 16 * k + 16)
            parts.append((piece.at[:, 80:96, 128 * k : 128 * k + 128], place.at[:, rows, 640:768]))
        for k, (source, where) in enumerate(parts):
            copies.append(pltpu.make_async_copy(source, where, sems.at[7 * i + k]))
    for copy in copies:
        copy.start()
    return copies


def early_kernel(sc_ref, query_ref, key_ref, value_ref, output_ref, down_ref, gains_ref, out_ref):
    core, member = sc_ref[0], sc_ref[2]
    for c, last in enumerate((key_ref, value_ref)):

        @pl.when(core == c)
        def _():
            for k in range(4):
                out_ref[k, 0:80, 0:512] = query_ref[:, 512 * c : 512 * c + 512]
                out_ref[k, 0:80, 512:640] = last[:, 0:128]
                for i in range(5):
                    out_ref[k, 80:96, 128 * i : 128 * i + 128] = last[16 * i : 16 * i + 16, 128:256]
                out_ref[k, 112:176, :] = output_ref[64 * c : 64 * c + 64, :]
                out_ref[k, 176:304, :] = down_ref[128 * c : 128 * c + 128, :]

    padded = jnp.concatenate([gains_ref[...], jnp.zeros((8, 512), F32)], axis=1)
    model = pltpu.roll(padded, member * 80, 1)
    head = pltpu.roll(padded, member * 32, 1)
    which = lax.broadcasted_iota(jnp.int32, (8, 640), 0)
    rows = jnp.concatenate([jnp.where(which < 4, model, head), jnp.zeros((8, 640), F32)], axis=0)
    for k in range(4):
        out_ref[k, 96:112, :] = rows.astype(BF16)


def late_kernel(sc_ref, gate_ref, up_ref, wide_out):
    core = sc_ref[0]
    for c in range(2):

        @pl.when(core == c)
        def _():
            for f in range(8):
                cols = slice(128 * f, 128 * f + 128)
                source = slice(256 * f + 128 * c, 256 * f + 128 * c + 128)
                wide_out[0, :, cols] = gate_ref[:, source]
                wide_out[1, :, cols] = up_ref[:, source]


def attend_kernel(
    sc_ref, tok_ref, prev_ref, cos_ref, sin_ref, pos_ref, near, far, near_t, far_t,
    q_ref, k_ref, v_ref, raw_ref, p_ref, mixed_ref, gains_ref, normed_ref, e_ref, sems,
):
    core, zl = sc_ref[0], sc_ref[1]
    copies = load_early((near, far, near_t, far_t), e_ref, core, zl, sems)
    unit, _ = normalize(tok_ref[...].astype(F32))
    unit_prev, _ = normalize(prev_ref[...].astype(F32))
    for copy in copies:
        copy.wait()
    gains = jnp.sum(e_ref[0, :, 80:96, 0:640].astype(F32), axis=0)
    gains_ref[...] = gains
    normed = (unit * gains[0:1, :640]).astype(BF16)
    normed_ref[...] = normed
    normed_prev = (unit_prev * gains[0:1, :640]).astype(BF16)
    g_query, g_key = gains[4:5, :256], gains[5:6, :256]
    mat_0 = e_ref[0, :, 0:80, :].reshape(640, 768)
    mat_1 = e_ref[1, :, 0:80, :].reshape(640, 768)
    raw_0 = product(normed, mat_0)
    raw_1 = product(normed, mat_1)
    raw_ref[:, 0:512] = raw_0[:, :512]
    raw_ref[:, 512:1024] = raw_1[:, :512]
    raw_ref[:, 1024:1280] = raw_0[:, 512:]
    v_ref[0:512, :] = product(normed_prev, mat_1[:, 512:]).astype(BF16)
    v_ref[512:1024, :] = raw_1[:, 512:].astype(BF16)
    prev_unit, _ = normalize(product(normed_prev, mat_0[:, 512:]))
    k_ref[0:512, :] = rotate(prev_unit * g_key, cos_ref[0:512, :], sin_ref[0:512, :]).astype(BF16)
    cosine, sine = cos_ref[512:1024, :], sin_ref[512:1024, :]
    own_unit, _ = normalize(raw_0[:, 512:])
    k_ref[512:1024, :] = rotate(own_unit * g_key, cosine, sine).astype(BF16)
    for h in range(HEADS):
        q_unit, _ = normalize(raw_ref[:, 256 * h : 256 * h + 256])
        turned = rotate(q_unit * g_query, cosine, sine).astype(BF16)
        q_ref[:, 256 * h : 256 * h + 256] = turned * BF16(SCALE)
    for b in range(2):
        rows = slice(256 * b, 256 * b + 256)
        keys = slice(256 * b, 256 * b + 768)
        query_at = lax.broadcasted_iota(jnp.int32, (256, 768), 0)
        key_at = lax.broadcasted_iota(jnp.int32, (256, 768), 1) - 512
        back = query_at - key_at
        allowed = (back >= 0) & (back < WINDOW) & (back <= pos_ref[rows, :])
        for h in range(HEADS):
            cols = slice(256 * h, 256 * h + 256)
            scores = jnp.where(allowed, product_rt(q_ref[rows, cols], k_ref[keys, :]), NEG)
            expd = jnp.exp(scores - jnp.max(scores, axis=-1, keepdims=True))
            probs = (expd / jnp.sum(expd, axis=-1, keepdims=True)).astype(BF16)
            p_ref[h, b] = probs
            mixed_ref[rows, cols] = product(probs, v_ref[keys, :]).astype(BF16)


def load_wide(pieces, target, zl, sems):
    copies = []
    for half, piece in enumerate(pieces):
        for near in range(2):
            group = zl if near == 0 else 1 - zl
            for k in range(2):
                place = target.at[k, half, pl.ds(group * 4, 4)]
                sem = sems.at[4 * half + 2 * near + k]
                copies.append(pltpu.make_async_copy(piece.at[:, near, k], place, sem))
    for copy in copies:
        copy.start()
    return copies


def load_out(pieces, out_w, core, zl, sems):
    copies = []
    for i, piece in enumerate(pieces):
        half = core if i < 2 else 1 - core
        group = zl if i % 2 == 0 else 1 - zl
        place = out_w.at[pl.ds(group * 4, 4), half]
        copies.append(pltpu.make_async_copy(piece.at[:, 0:64], place, sems.at[i]))
    for copy in copies:
        copy.start()
    return copies


def load_down(pieces, down_w, zl, sems):
    copies = []
    for i, piece in enumerate(pieces):
        group = zl if i % 2 == 0 else 1 - zl
        place = down_w.at[i // 2, pl.ds(group * 4, 4)]
        copies.append(pltpu.make_async_copy(piece.at[:, 64:192], place, sems.at[i]))
    for copy in copies:
        copy.start()
    return copies


def forward_kernel(
    sc_ref, mixed_ref, tok_ref, cot_ref, gains_ref, w0, w1, t0, t1, t2, t3,
    out_ref, branch_ref, middle_ref, nm_ref, act_ref, slope_ref, gd_ref, hid_own_ref, other_ref, gain_ref,
    wide_w, out_w, down_w, hid_other_ref, wide_sems, out_sems, down_sems,
):
    core, zl = sc_ref[0], sc_ref[1]
    tall = load_out((t0, t1, t2, t3), out_w, core, zl, out_sems)
    wide = load_wide((w0, w1), wide_w, zl, wide_sems)
    wide += load_down((t0, t1, t2, t3), down_w, zl, down_sems)
    hid_refs = (hid_own_ref, hid_other_ref)
    for copy in tall:
        copy.wait()
    g_mixed, g_hidden, g_final = [gains_ref[i : i + 1, :640] for i in (1, 2, 3)]
    out_mat = out_w[...].reshape(1024, 640)
    branch_ref[...] = product(mixed_ref[...], out_mat)
    for copy in wide:
        copy.wait()
    gain_sum = jnp.zeros((1, 640), F32)
    for b in range(2):
        rows = slice(256 * b, 256 * b + 256)
        branch_unit, _ = normalize(branch_ref[rows, :])
        middle = tok_ref[rows, :].astype(F32) + branch_unit * g_mixed
        middle_ref[rows, :] = middle
        mid_unit, _ = normalize(middle)
        normed = (mid_unit * g_hidden).astype(BF16)
        nm_ref[rows, :] = normed
        down = jnp.zeros((256, 640), F32)
        for half in range(2):
            for n in range(2):
                cols = slice(512 * n, 512 * n + 512)
                u = product(normed, wide_w[0, half, :, :, cols].reshape(640, 512))
                upward = product(normed, wide_w[1, half, :, :, cols].reshape(640, 512))
                square = u * u
                t = jnp.tanh(GELU_A * u * (1.0 + GELU_B * square))
                side = 0.5 * (1.0 + t)
                active = u * side
                slope = side + 0.5 * u * (1.0 - t * t) * (GELU_A * (1.0 + 3.0 * GELU_B * square))
                act_ref[half, rows, cols] = active.astype(BF16)
                slope_ref[half, rows, cols] = (slope * upward).astype(BF16)
                hidden = (active * upward).astype(BF16)
                hid_refs[half][rows, cols] = hidden
                mat = down_w[half, 4 * n : 4 * n + 4].reshape(512, 640)
                down = down + product(hidden, mat)
        down_unit, down_factor = normalize(down)
        out_ref[rows, :] = middle + down_unit * g_final
        grad_out = cot_ref[rows, :].astype(F32)
        gain_sum = gain_sum + column_sum(grad_out * down_unit)
        gd_ref[rows, :] = norm_back(grad_out * g_final, down_unit, down_factor).astype(BF16)
    gain_ref[...] = gain_sum
    down_blocks(hid_other_ref, gd_ref, None, other_ref)


def down_blocks(hid_ref, gd_ref, received, ref):
    for n in range(2):
        members = slice(4 * n, 4 * n + 4)
        part = product_lt(hid_ref[:, 512 * n : 512 * n + 512], gd_ref[...]).reshape(4, 8, 16, 640)
        for i in range(8):
            for j in range(5):
                block = part[:, i, :, 128 * j : 128 * j + 128]
                if received is not None:
                    block = block + received[members, 5 * i + j].astype(F32)
                ref[members, 5 * i + j] = block.astype(BF16)


def wide_blocks(nm_ref, grad_ref, received, ref, start):
    for n in range(2):
        part = product_lt(nm_ref[...], grad_ref[:, 512 * n : 512 * n + 512]).reshape(8, 5, 16, 512)
        for i in range(5):
            for j in range(4):
                at = 8 * i + 4 * n + j
                block = part[:, i, :, 128 * j : 128 * j + 128]
                if received is not None:
                    block = block + received[:, at].astype(F32)
                ref[:, start + at] = block.astype(BF16)


def first_sums_kernel(hid_ref, gd_ref, nm_ref, gg_ref, down_received, gate_received, ref):
    down_blocks(hid_ref, gd_ref, down_received, ref)
    wide_blocks(nm_ref, gg_ref, gate_received, ref, 40)


def second_sums_kernel(nm_ref, gu_ref, up_received, out_own, out_received, ref):
    wide_blocks(nm_ref, gu_ref, up_received, ref, 0)
    for at in range(20):
        block = out_own[:, at].astype(F32) + out_received[:, at].astype(F32)
        ref[:, 40 + at] = block.astype(BF16)
    ref[:, 60:64] = jnp.zeros((8, 4, 16, 128), BF16)


def backward_kernel(
    sc_ref, act_ref, slope_ref, gd_ref, nm_ref, mixed_ref, cot_ref, gains_ref, branch_ref, middle_ref,
    w0, w1, t0, t1, t2, t3,
    gg_own_ref, gu_own_ref, gate_other_ref, up_other_ref, gmid_ref, gmixed_ref, own_ref, other_ref, gain_ref,
    gg_other_ref, gu_other_ref, wide_w, out_w, down_w, gb_ref, split_ref, wide_sems, out_sems, down_sems,
):
    core, zl = sc_ref[0], sc_ref[1]
    down = load_down((t0, t1, t2, t3), down_w, sc_ref[1], down_sems)
    wide = load_wide((w0, w1), wide_w, zl, wide_sems)
    wide += load_out((t0, t1, t2, t3), out_w, core, zl, out_sems)
    for copy in down:
        copy.wait()
    for half, (gg_ref, gu_ref) in enumerate(((gg_own_ref, gu_own_ref), (gg_other_ref, gu_other_ref))):
        for n in range(2):
            cols = slice(512 * n, 512 * n + 512)
            mat = down_w[half, 4 * n : 4 * n + 4].reshape(512, 640)
            grad_hidden = product_rt(gd_ref[...], mat)
            gg_ref[:, cols] = (grad_hidden * slope_ref[half, :, cols].astype(F32)).astype(BF16)
            gu_ref[:, cols] = (grad_hidden * act_ref[half, :, cols].astype(F32)).astype(BF16)
    wide_blocks(nm_ref, gg_other_ref, None, gate_other_ref, 0)
    wide_blocks(nm_ref, gu_other_ref, None, up_other_ref, 0)
    for copy in wide:
        copy.wait()
    g_mixed, g_hidden = [gains_ref[i : i + 1, :640] for i in (1, 2)]
    sum_mixed = jnp.zeros((1, 640), F32)
    sum_hidden = jnp.zeros((1, 640), F32)
    for b in range(2):
        rows = slice(256 * b, 256 * b + 256)
        grad_normed = jnp.zeros((256, 640), F32)
        for half, refs in enumerate(((gg_own_ref, gu_own_ref), (gg_other_ref, gu_other_ref))):
            for at, ref in enumerate(refs):
                grad_normed = grad_normed + product_rt(
                    ref[rows, :], wide_w[at, half].reshape(640, 1024)
                )
        mid_unit, mid_factor = normalize(middle_ref[rows, :])
        sum_hidden = sum_hidden + column_sum(grad_normed * mid_unit)
        grad_middle = cot_ref[rows, :].astype(F32) + norm_back(
            grad_normed * g_hidden, mid_unit, mid_factor
        )
        gmid_ref[rows, :] = grad_middle
        branch_unit, branch_factor = normalize(branch_ref[rows, :])
        sum_mixed = sum_mixed + column_sum(grad_middle * branch_unit)
        grad_branch = norm_back(grad_middle * g_mixed, branch_unit, branch_factor).astype(BF16)
        gb_ref[rows, :] = grad_branch
        gmixed_ref[rows, :] = product_rt(grad_branch, out_w[...].reshape(1024, 640)).astype(BF16)
    gain_ref[0:1, :] = sum_mixed
    gain_ref[1:2, :] = sum_hidden
    for n in range(2):
        part = product_lt(mixed_ref[:, 512 * n : 512 * n + 512], gb_ref[...])
        part = part.astype(BF16).reshape(4, 2, 4, 16, 640)
        for c in range(2):
            split_ref[c, 4 * n : 4 * n + 4] = part[:, c]
    for half, ref in ((core, own_ref), (1 - core, other_ref)):
        part = split_ref[half]
        for i in range(4):
            for j in range(5):
                ref[:, i * 5 + j] = part[:, i, :, 128 * j : 128 * j + 128]


def attend_back_kernel(
    q_ref, k_ref, v_ref, p_ref, gm_ref, gq_ref, far_k_ref, far_v_ref, own_k_ref, own_v_ref, dk_ref, dv_ref
):
    dk_ref[...] = jnp.zeros((1024, 256), F32)
    dv_ref[...] = jnp.zeros((1024, 256), F32)
    for b in range(2):
        rows = slice(256 * b, 256 * b + 256)
        keys = slice(256 * b, 256 * b + 768)
        for h in range(HEADS):
            cols = slice(256 * h, 256 * h + 256)
            probs = p_ref[h, b]
            grads = gm_ref[rows, cols]
            weighed = probs.astype(F32)
            grad_probs = product_rt(grads, v_ref[keys, :])
            inner = jnp.sum(weighed * grad_probs, axis=-1, keepdims=True)
            grad_scores = (weighed * (grad_probs - inner)).astype(BF16)
            gq_ref[rows, cols] = product(grad_scores, k_ref[keys, :]) * SCALE
            dk_ref[keys, :] += product_lt(grad_scores, q_ref[rows, cols])
            dv_ref[keys, :] += product_lt(probs, grads)
    far_k_ref[...] = dk_ref[0:512, :].astype(BF16)
    far_v_ref[...] = dv_ref[0:512, :].astype(BF16)
    own_k_ref[...] = dk_ref[512:1024, :]
    own_v_ref[...] = dv_ref[512:1024, :]


def query_back_kernel(gq_ref, raw_ref, cos_ref, sin_ref, gains_ref, e_ref, low_ref, gn_ref, gain_ref):
    cosine, sine = cos_ref[512:1024, :], sin_ref[512:1024, :]
    g_query = gains_ref[4:5, :256]
    total = jnp.zeros((1, 256), F32)
    for h in range(HEADS):
        cols = slice(256 * h, 256 * h + 256)
        turned = rotate(gq_ref[:, cols], cosine, -sine)
        unit, factor = normalize(raw_ref[:, cols])
        total = total + column_sum(turned * unit)
        low_ref[:, cols] = norm_back(turned * g_query, unit, factor).astype(BF16)
    gain_ref[...] = total
    gn_ref[...] = product_rt(
        low_ref[:, 0:512], e_ref[0, :, 0:80, 0:512].reshape(640, 512)
    ) + product_rt(low_ref[:, 512:1024], e_ref[1, :, 0:80, 0:512].reshape(640, 512))


def early_blocks(heads, last, normed_ref, received, ref):
    for grads, at in ((heads, 0), (last, 4)):
        part = product_lt(normed_ref[...], grads).reshape(8, 5, 16, grads.shape[1])
        for i in range(5):
            for j in range(grads.shape[1] // 128):
                block = part[:, i, :, 128 * j : 128 * j + 128]
                if received is not None:
                    block = block + received[:, i * 6 + at + j].astype(F32)
                ref[:, i * 6 + at + j] = block.astype(BF16)


def key_back_kernel(
    sc_ref, normed_ref, low_ref, own_k_ref, own_v_ref, back_k_ref, back_v_ref, raw_ref, cos_ref, sin_ref,
    gains_ref, gk_ref, gv_ref, other_ref, gain_ref,
):
    other = 1 - sc_ref[0]
    cosine, sine = cos_ref[512:1024, :], sin_ref[512:1024, :]
    key_grad = own_k_ref[...] + back_k_ref[...].astype(F32)
    gv_ref[...] = (own_v_ref[...] + back_v_ref[...].astype(F32)).astype(BF16)
    turned = rotate(key_grad, cosine, -sine)
    unit, factor = normalize(raw_ref[:, 1024:1280])
    gain_ref[...] = column_sum(turned * unit)
    gk_ref[...] = norm_back(turned * gains_ref[5:6, :256], unit, factor).astype(BF16)
    last = jnp.where(other == 0, gk_ref[...].astype(F32), gv_ref[...].astype(F32)).astype(BF16)
    heads = low_ref[:, pl.ds(pl.multiple_of(other * 512, 512), 512)]
    early_blocks(heads, last, normed_ref, None, other_ref)


def token_back_kernel(
    tok_ref, gn_ref, gk_ref, gv_ref, gains_ref, e_ref, gmid_ref, gtok_ref, gain_ref
):
    grad_normed = (
        gn_ref[...]
        + product_rt(gk_ref[...], e_ref[0, :, 0:80, 512:768].reshape(640, 256))
        + product_rt(gv_ref[...], e_ref[1, :, 0:80, 512:768].reshape(640, 256))
    )
    unit_in, factor_in = normalize(tok_ref[...].astype(F32))
    gain_ref[...] = column_sum(grad_normed * unit_in)
    gtok_ref[...] = gmid_ref[...] + norm_back(grad_normed * gains_ref[0:1, :640], unit_in, factor_in)


def early_own_kernel(
    sc_ref, normed_ref, low_ref, gk_ref, gv_ref, received, gain_i_ref, gain_b_ref, gain_f_ref, gain_q_ref,
    gain_k_ref, ref, rows_ref,
):
    core = sc_ref[0]
    last = jnp.where(core == 0, gk_ref[...].astype(F32), gv_ref[...].astype(F32)).astype(BF16)
    heads = low_ref[:, pl.ds(pl.multiple_of(core * 512, 512), 512)]
    early_blocks(heads, last, normed_ref, received, ref)
    rows_ref[...] = jnp.zeros((32, 128), F32)
    spans = (
        (gain_i_ref[...], 0, 5),
        (gain_b_ref[0:1, :], 5, 5),
        (gain_b_ref[1:2, :], 10, 5),
        (gain_f_ref[...], 15, 5),
        (gain_q_ref[...], 20, 2),
        (gain_k_ref[...], 22, 2),
    )
    for vector, start, count in spans:
        for j in range(count):
            rows_ref[start + j : start + j + 1, :] = vector[:, 128 * j : 128 * j + 128]
    blocks = rows_ref[...].astype(BF16).reshape(2, 16, 128)
    for f in range(8):
        ref[f, 30:32] = blocks


def unpack_kernel(
    sc_ref, mine_ref, theirs_ref,
    gq_ref, gk_ref, gv_ref, gout_ref, ggate_ref, gup_ref, gdown_ref,
    gain_0, gain_1, gain_2, gain_3, gain_4, gain_5, both_ref,
):
    core = sc_ref[0]
    both_ref[core] = mine_ref[...]
    both_ref[1 - core] = theirs_ref[...]

    def block(c, kind, at):
        base, per = {"first": (0, 10), "second": (160, 8), "early": (288, 4)}[kind]
        start = base + 16 * (at % per)
        return both_ref[c, at // per, start : start + 16, :].astype(F32)

    for c in range(2):
        for i in range(5):
            rows = slice(16 * i, 16 * i + 16)
            for j in range(8):
                cols = slice(256 * j + 128 * c, 256 * j + 128 * c + 128)
                ggate_ref[rows, cols] = block(c, "first", 40 + 8 * i + j)
                gup_ref[rows, cols] = block(c, "second", 8 * i + j)
            for j in range(4):
                gq_ref[rows, 512 * c + 128 * j : 512 * c + 128 * j + 128] = block(c, "early", 6 * i + j)
            for j in range(2):
                (gk_ref, gv_ref)[c][rows, 128 * j : 128 * j + 128] = block(c, "early", 6 * i + 4 + j)
        for i in range(8):
            for j in range(5):
                cols = slice(128 * j, 128 * j + 128)
                gdown_ref[128 * c + 16 * i : 128 * c + 16 * i + 16, cols] = block(c, "first", 5 * i + j)
                if i < 4:
                    gout_ref[64 * c + 16 * i : 64 * c + 16 * i + 16, cols] = block(
                        c, "second", 40 + 5 * i + j
                    )
    rows = jnp.concatenate(
        [block(0, "early", at) + block(1, "early", at) for at in (30, 31)], axis=0
    )
    member = sc_ref[2]
    for i, (start, count, size) in enumerate(
        ((0, 5, 80), (5, 5, 80), (10, 5, 80), (15, 5, 80), (20, 2, 32), (22, 2, 32))
    ):
        line = jnp.concatenate([rows[start + j : start + j + 1, :] for j in range(count)], axis=1)
        line = jnp.broadcast_to(line, (8, 128 * count))
        turned = pltpu.roll(line, lax.rem(128 * count - member * size, 128 * count), 1)
        (gain_0, gain_1, gain_2, gain_3, gain_4, gain_5)[i][...] = turned[0:1, 0:size]


def on_device(
    tokens,
    positions,
    cotangent,
    query_weight,
    key_weight,
    value_weight,
    output_weight,
    gate_weight,
    upward_weight,
    down_weight,
    gain_input,
    gain_mixed,
    gain_hidden,
    gain_final,
    gain_query,
    gain_key,
):
    core = lax.axis_index("core")
    member = lax.axis_index(FSDP)
    scalars = jnp.stack([core, lax.axis_index("zl"), member]).astype(jnp.int32)

    gain_rows = jnp.concatenate(
        [
            jnp.pad(gain, (0, 128 - gain.shape[0]))[None, :]
            for gain in (gain_input, gain_mixed, gain_hidden, gain_final, gain_query, gain_key)
        ]
        + [jnp.zeros((2, 128), BF16)]
    ).astype(F32)
    early_spread = call(
        early_kernel,
        (scalars, query_weight, key_weight, value_weight, output_weight, down_weight, gain_rows),
        [SMEM] + [VMEM] * 6,
        [shape((4, 304, 640), BF16)],
    )[0]
    wide = call(
        late_kernel, (scalars, gate_weight, upward_weight), [SMEM] + [VMEM] * 2, [shape((2, 80, 1024), BF16)]
    )[0]
    prev = passed_along(tokens, 1)
    wide_far = along_z(wide, 1)
    near = along_y(early_spread)
    wide_own = along_y(pair_spread(wide, after(wide_far, (near, prev))))
    early_near, tall_near = near[:, :112], near[:, 112:]
    early_far = along_z(early_near, 3)
    early_parts = (early_near, early_far, swapped(early_near), swapped(early_far))
    tall_far = along_z(tall_near, 1)
    tall_parts = (tall_near, tall_far, swapped(tall_near), swapped(tall_far))

    before = positions[0] - ROWS + jnp.arange(ROWS, dtype=jnp.int32)
    freqs = THETA ** (-(jnp.arange(HEAD // 2, dtype=F32) * 2.0) / HEAD)
    phase = jnp.concatenate([before, positions]).astype(F32)[:, None] * freqs[None, :]
    cosine, sine = jnp.cos(phase), jnp.sin(phase)

    queries, keys, values, raw, probs, mixed, gains, normed, mats = call(
        attend_kernel,
        (scalars, tokens, prev, cosine, sine, positions[:, None]) + early_parts,
        [SMEM] + [VMEM] * 5 + [ANY] * 4,
        [
            shape((512, 1024), BF16),
            shape((1024, 256), BF16),
            shape((1024, 256), BF16),
            shape((512, 1280), F32),
            shape((4, 2, 256, 768), BF16),
            shape((512, 1024), BF16),
            shape((16, 640), F32),
            shape((512, 640), BF16),
            shape((2, 8, 96, 768), BF16),
        ],
        [pltpu.SemaphoreType.DMA((28,))],
        us=9,
    )
    wide_own = after(wide_own, (mixed,) + tall_parts)
    wide_parts = (wide_own, swapped(wide_own))
    wide_scratch = pltpu.VMEM((2, 2, 8, 80, 1024), BF16)
    out_scratch = pltpu.VMEM((8, 2, 64, 640), BF16)
    down_scratch = pltpu.VMEM((2, 8, 128, 640), BF16)
    sems_4, sems_8 = pltpu.SemaphoreType.DMA((4,)), pltpu.SemaphoreType.DMA((8,))
    layer_out, branch, middle, normed_mid, active, slope, grad_down, hid_own, down_other, gain_f = call(
        forward_kernel,
        (scalars, mixed, tokens, cotangent, gains) + wide_parts + tall_parts,
        [SMEM] + [VMEM] * 4 + [ANY] * 6,
        [
            shape((512, 640), F32),
            shape((512, 640), F32),
            shape((512, 640), F32),
            shape((512, 640), BF16),
            shape((2, 512, 1024), BF16),
            shape((2, 512, 1024), BF16),
            shape((512, 640), BF16),
            shape((512, 1024), BF16),
            shape((8, 40, 16, 128), BF16),
            shape((1, 640), F32),
        ],
        [wide_scratch, out_scratch, down_scratch, pltpu.VMEM((512, 1024), BF16), sems_8, sems_4, sems_4],
        us=13,
    )
    down_received = swapped(down_other)
    gg_own, gu_own, gate_other, up_other, grad_middle, grad_mixed, out_own, out_other, gain_b = call(
        backward_kernel,
        (
            scalars, active, slope, grad_down, normed_mid, mixed, cotangent, gains, branch,
            middle,
        )
        + wide_parts
        + tall_parts,
        [SMEM] + [VMEM] * 9 + [ANY] * 6,
        [
            shape((512, 1024), BF16),
            shape((512, 1024), BF16),
            shape((8, 40, 16, 128), BF16),
            shape((8, 40, 16, 128), BF16),
            shape((512, 640), F32),
            shape((512, 1024), BF16),
            shape((8, 20, 16, 128), BF16),
            shape((8, 20, 16, 128), BF16),
            shape((2, 640), F32),
        ],
        [
            pltpu.VMEM((512, 1024), BF16),
            pltpu.VMEM((512, 1024), BF16),
            wide_scratch,
            out_scratch,
            down_scratch,
            pltpu.VMEM((512, 640), BF16),
            pltpu.VMEM((2, 8, 4, 16, 640), BF16),
            sems_8,
            sems_4,
            sems_4,
        ],
        us=17,
    )
    first_sum = call(
        first_sums_kernel,
        (hid_own, grad_down, normed_mid, gg_own, down_received, swapped(gate_other)),
        [VMEM] * 6,
        [shape((8, 80, 16, 128), BF16)],
        us=6,
    )[0]
    first_part = chips_sum(first_sum.reshape(64, 160, 128))
    grad_mixed = after(grad_mixed, first_sum)
    grad_queries, far_k, far_v, own_k, own_v = call(
        attend_back_kernel,
        (queries, keys, values, probs, grad_mixed),
        [VMEM] * 5,
        [
            shape((512, 1024), F32),
            shape((512, 256), BF16),
            shape((512, 256), BF16),
            shape((512, 256), F32),
            shape((512, 256), F32),
        ],
        [pltpu.VMEM((1024, 256), F32), pltpu.VMEM((1024, 256), F32)],
        us=6,
    )
    back_k = passed_along(far_k, -1)
    back_v = passed_along(far_v, -1)
    second_sum = call(
        second_sums_kernel,
        (after(normed_mid, far_k), gu_own, swapped(up_other), out_own, swapped(out_other)),
        [VMEM] * 5,
        [shape((8, 64, 16, 128), BF16)],
        us=4,
    )[0]
    second_part = chips_sum(after(second_sum.reshape(64, 128, 128), (first_part, back_k, back_v)))
    low_query, grad_normed, gain_q = call(
        query_back_kernel,
        (grad_queries, raw, cosine, sine, gains, mats),
        [VMEM] * 6,
        [shape((512, 1024), BF16), shape((512, 640), F32), shape((1, 256), F32)],
    )
    small = shape((512, 256), BF16)
    grad_key, grad_value, early_other, gain_k = call(
        key_back_kernel,
        (scalars, normed, low_query, own_k, own_v, back_k, back_v, raw, cosine, sine, gains),
        [SMEM] + [VMEM] * 10,
        [small, small, shape((8, 30, 16, 128), BF16), shape((1, 256), F32)],
    )
    early_received = swapped(early_other)
    grad_tokens, gain_i = call(
        token_back_kernel,
        (tokens, grad_normed, grad_key, grad_value, gains, mats, grad_middle),
        [VMEM] * 7,
        [shape((512, 640), F32), shape((1, 640), F32)],
    )
    early_sum = call(
        early_own_kernel,
        (
            scalars, normed, low_query, grad_key, grad_value, early_received, gain_i, gain_b, gain_f, gain_q,
            gain_k,
        ),
        [SMEM] + [VMEM] * 10,
        [shape((8, 32, 16, 128), BF16)],
        [pltpu.VMEM((32, 128), F32)],
    )[0]
    early_part = chips_sum(after(early_sum.reshape(64, 64, 128), second_part))
    part = jnp.concatenate([first_part, second_part, early_part], axis=0)
    mine_all = lax.all_to_all(
        jnp.broadcast_to(part[None], (8, 352, 128)), ("x", "zh"), 0, 0, tiled=True
    )
    theirs_all = swapped(mine_all)
    grads = call(
        unpack_kernel,
        (scalars, mine_all, theirs_all),
        [SMEM, VMEM, VMEM],
        [
            shape((80, 1024), F32),
            shape((80, 256), F32),
            shape((80, 256), F32),
            shape((128, 640), F32),
            shape((80, 2048), F32),
            shape((80, 2048), F32),
            shape((256, 640), F32),
            *[shape((1, size), F32) for size in (80, 80, 80, 80, 32, 32)],
        ],
        [pltpu.VMEM((2, 8, 352, 128), BF16)],
    )
    gain_grads = [grad.reshape(-1) for grad in grads[7:]]
    return (layer_out, grad_tokens, *grads[:7], *gain_grads)


def solution(mesh):
    fine = Mesh(mesh.devices.reshape(4, 2, 2, 2, 4), REP + FSDP)
    rows = P(REP + FSDP, None)
    weight = P(FSDP, None)
    gain = P(FSDP)
    in_specs = (rows, P(REP + FSDP), rows) + (weight,) * 7 + (gain,) * 6
    out_specs = (rows, rows) + (weight,) * 7 + (gain,) * 6
    return jax.shard_map(
        on_device, mesh=fine, in_specs=in_specs, out_specs=out_specs, check_vma=False
    )
```

```python
import jax
import jax.numpy as jnp
from jax import lax
from jax.experimental import pallas as pl
from jax.experimental.pallas import tpu as pltpu
from jax.sharding import Mesh
from jax.sharding import PartitionSpec as P

HEADS = 4
HEAD = 256
WINDOW = 512
ROWS = 512
EPS = 1e-06
THETA = 10000.0
SCALE = 0.0625
NEG = -1e30
GELU_A = 0.7978845608028654
GELU_B = 0.044715

REP = ("x", "zh", "core")
FSDP = ("zl", "y")
BF16 = jnp.bfloat16
F32 = jnp.float32
ANY = pl.BlockSpec(memory_space=pl.ANY)
VMEM = pl.BlockSpec(memory_space=pltpu.VMEM)
SMEM = pl.BlockSpec(memory_space=pltpu.SMEM)


def shape(dims, dtype):
    return jax.ShapeDtypeStruct(dims, dtype)


def call(kernel, ins, in_specs, outs, scratch=(), room=60, us=2):
    return pl.pallas_call(
        kernel,
        out_shape=outs,
        in_specs=in_specs,
        out_specs=[VMEM] * len(outs),
        scratch_shapes=list(scratch),
        compiler_params=pltpu.CompilerParams(vmem_limit_bytes=room * 1024 * 1024),
        cost_estimate=pl.CostEstimate(
            flops=us * 1_150_000_000, bytes_accessed=1, transcendentals=0
        ),
    )(*ins)


def passed_along(value, steps):
    initial, last = (max(0, -steps), min(8, 8 - steps))
    pairs = [(source, source + steps) for source in range(initial, last)]
    return lax.ppermute(value, FSDP, pairs)


def swapped(value):
    return lax.ppermute(value, "core", [(0, 1), (1, 0)])


def along_y(spread):
    return lax.all_to_all(spread, "y", 0, 0, tiled=True)


def along_z(value, steps):
    return lax.ppermute(value, ("zh", "zl"), [(i, (i + steps) % 4) for i in range(4)])


def pair_spread(near, far):
    return jnp.broadcast_to(jnp.stack([near, far])[None], (4, 2) + near.shape)


def after(value, earlier):
    return lax.optimization_barrier((value, earlier))[0]


def chips_sum(both):
    parts = lax.all_to_all(both, ("zl", "y", "x", "zh"), 0, 0, tiled=True)
    return jnp.sum(parts.astype(F32), axis=0).astype(BF16)


def normalize(values):
    factor = lax.rsqrt(jnp.mean(values * values, axis=-1, keepdims=True) + EPS)
    return (values * factor, factor)


def norm_back(grad_hat, unit, factor):
    return factor * (grad_hat - unit * jnp.mean(grad_hat * unit, axis=-1, keepdims=True))


def rotate(values, cosine, sine):
    first, second = values[:, :128], values[:, 128:]
    return jnp.concatenate(
        [first * cosine - second * sine, second * cosine + first * sine], axis=-1
    )


def product(left, right):
    return jnp.dot(left, right, preferred_element_type=F32)


def product_rt(left, right):
    return lax.dot_general(left, right, (((1,), (1,)), ((), ())), preferred_element_type=F32)


def product_lt(left, right):
    return lax.dot_general(left, right, (((0,), (0,)), ((), ())), preferred_element_type=F32)


def column_sum(values):
    return jnp.sum(values, axis=0, keepdims=True)


def load_early(pieces, target, core, zl, sems):
    copies = []
    for i, piece in enumerate(pieces):
        half = core if i < 2 else 1 - core
        group = zl if i % 2 == 0 else 1 - zl
        place = target.at[half, pl.ds(group * 4, 4)]
        parts = [(piece.at[:, 0:80], place.at[:, 0:80, 0:640]), (piece.at[:, 96:112], place.at[:, 80:96, 0:640])]
        for k in range(5):
            rows = slice(16 * k, 16 * k + 16)
            parts.append((piece.at[:, 80:96, 128 * k : 128 * k + 128], place.at[:, rows, 640:768]))
        for k, (source, where) in enumerate(parts):
            copies.append(pltpu.make_async_copy(source, where, sems.at[7 * i + k]))
    for copy in copies:
        copy.start()
    return copies


def early_kernel(sc_ref, query_ref, key_ref, value_ref, output_ref, down_ref, gains_ref, out_ref):
    core, member = sc_ref[0], sc_ref[2]
    for c, last in enumerate((key_ref, value_ref)):

        @pl.when(core == c)
        def _():
            for k in range(4):
                out_ref[k, 0:80, 0:512] = query_ref[:, 512 * c : 512 * c + 512]
                out_ref[k, 0:80, 512:640] = last[:, 0:128]
                for i in range(5):
                    out_ref[k, 80:96, 128 * i : 128 * i + 128] = last[16 * i : 16 * i + 16, 128:256]
                out_ref[k, 112:176, :] = output_ref[64 * c : 64 * c + 64, :]
                out_ref[k, 176:304, :] = down_ref[128 * c : 128 * c + 128, :]

    padded = jnp.concatenate([gains_ref[...], jnp.zeros((8, 512), F32)], axis=1)
    model = pltpu.roll(padded, member * 80, 1)
    head = pltpu.roll(padded, member * 32, 1)
    which = lax.broadcasted_iota(jnp.int32, (8, 640), 0)
    rows = jnp.concatenate([jnp.where(which < 4, model, head), jnp.zeros((8, 640), F32)], axis=0)
    for k in range(4):
        out_ref[k, 96:112, :] = rows.astype(BF16)


def late_kernel(sc_ref, gate_ref, up_ref, wide_out):
    core = sc_ref[0]
    for c in range(2):

        @pl.when(core == c)
        def _():
            for f in range(8):
                cols = slice(128 * f, 128 * f + 128)
                source = slice(256 * f + 128 * c, 256 * f + 128 * c + 128)
                wide_out[0, :, cols] = gate_ref[:, source]
                wide_out[1, :, cols] = up_ref[:, source]


def attend_kernel(
    sc_ref, tok_ref, prev_ref, cos_ref, sin_ref, pos_ref, near, far, near_t, far_t,
    q_ref, k_ref, v_ref, raw_ref, p_ref, mixed_ref, gains_ref, normed_ref, e_ref, sems,
):
    core, zl = sc_ref[0], sc_ref[1]
    copies = load_early((near, far, near_t, far_t), e_ref, core, zl, sems)
    unit, _ = normalize(tok_ref[...].astype(F32))
    unit_prev, _ = normalize(prev_ref[...].astype(F32))
    for copy in copies:
        copy.wait()
    gains = jnp.sum(e_ref[0, :, 80:96, 0:640].astype(F32), axis=0)
    gains_ref[...] = gains
    normed = (unit * gains[0:1, :640]).astype(BF16)
    normed_ref[...] = normed
    normed_prev = (unit_prev * gains[0:1, :640]).astype(BF16)
    g_query, g_key = gains[4:5, :256], gains[5:6, :256]
    mat_0 = e_ref[0, :, 0:80, :].reshape(640, 768)
    mat_1 = e_ref[1, :, 0:80, :].reshape(640, 768)
    raw_0 = product(normed, mat_0)
    raw_1 = product(normed, mat_1)
    raw_ref[:, 0:512] = raw_0[:, :512]
    raw_ref[:, 512:1024] = raw_1[:, :512]
    raw_ref[:, 1024:1280] = raw_0[:, 512:]
    v_ref[0:512, :] = product(normed_prev, mat_1[:, 512:]).astype(BF16)
    v_ref[512:1024, :] = raw_1[:, 512:].astype(BF16)
    prev_unit, _ = normalize(product(normed_prev, mat_0[:, 512:]))
    k_ref[0:512, :] = rotate(prev_unit * g_key, cos_ref[0:512, :], sin_ref[0:512, :]).astype(BF16)
    cosine, sine = cos_ref[512:1024, :], sin_ref[512:1024, :]
    own_unit, _ = normalize(raw_0[:, 512:])
    k_ref[512:1024, :] = rotate(own_unit * g_key, cosine, sine).astype(BF16)
    for h in range(HEADS):
        q_unit, _ = normalize(raw_ref[:, 256 * h : 256 * h + 256])
        turned = rotate(q_unit * g_query, cosine, sine).astype(BF16)
        q_ref[:, 256 * h : 256 * h + 256] = turned * BF16(SCALE)
    for b in range(2):
        rows = slice(256 * b, 256 * b + 256)
        keys = slice(256 * b, 256 * b + 768)
        query_at = lax.broadcasted_iota(jnp.int32, (256, 768), 0)
        key_at = lax.broadcasted_iota(jnp.int32, (256, 768), 1) - 512
        back = query_at - key_at
        allowed = (back >= 0) & (back < WINDOW) & (back <= pos_ref[rows, :])
        for h in range(HEADS):
            cols = slice(256 * h, 256 * h + 256)
            scores = jnp.where(allowed, product_rt(q_ref[rows, cols], k_ref[keys, :]), NEG)
            expd = jnp.exp(scores - jnp.max(scores, axis=-1, keepdims=True))
            probs = (expd / jnp.sum(expd, axis=-1, keepdims=True)).astype(BF16)
            p_ref[h, b] = probs
            mixed_ref[rows, cols] = product(probs, v_ref[keys, :]).astype(BF16)


def load_wide(pieces, target, zl, sems):
    copies = []
    for half, piece in enumerate(pieces):
        for near in range(2):
            group = zl if near == 0 else 1 - zl
            for k in range(2):
                place = target.at[k, half, pl.ds(group * 4, 4)]
                sem = sems.at[4 * half + 2 * near + k]
                copies.append(pltpu.make_async_copy(piece.at[:, near, k], place, sem))
    for copy in copies:
        copy.start()
    return copies


def load_out(pieces, out_w, core, zl, sems):
    copies = []
    for i, piece in enumerate(pieces):
        half = core if i < 2 else 1 - core
        group = zl if i % 2 == 0 else 1 - zl
        place = out_w.at[pl.ds(group * 4, 4), half]
        copies.append(pltpu.make_async_copy(piece.at[:, 0:64], place, sems.at[i]))
    for copy in copies:
        copy.start()
    return copies


def load_down(pieces, down_w, zl, sems):
    copies = []
    for i, piece in enumerate(pieces):
        group = zl if i % 2 == 0 else 1 - zl
        place = down_w.at[i // 2, pl.ds(group * 4, 4)]
        copies.append(pltpu.make_async_copy(piece.at[:, 64:192], place, sems.at[i]))
    for copy in copies:
        copy.start()
    return copies


def forward_kernel(
    sc_ref, mixed_ref, tok_ref, cot_ref, gains_ref, w0, w1, t0, t1, t2, t3,
    out_ref, branch_ref, middle_ref, nm_ref, act_ref, slope_ref, gd_ref, hid_own_ref, other_ref, gain_ref,
    wide_w, out_w, down_w, hid_other_ref, wide_sems, out_sems, down_sems,
):
    core, zl = sc_ref[0], sc_ref[1]
    tall = load_out((t0, t1, t2, t3), out_w, core, zl, out_sems)
    wide = load_wide((w0, w1), wide_w, zl, wide_sems)
    wide += load_down((t0, t1, t2, t3), down_w, zl, down_sems)
    hid_refs = (hid_own_ref, hid_other_ref)
    for copy in tall:
        copy.wait()
    g_mixed, g_hidden, g_final = [gains_ref[i : i + 1, :640] for i in (1, 2, 3)]
    out_mat = out_w[...].reshape(1024, 640)
    branch_ref[...] = product(mixed_ref[...], out_mat)
    for copy in wide:
        copy.wait()
    gain_sum = jnp.zeros((1, 640), F32)
    for b in range(2):
        rows = slice(256 * b, 256 * b + 256)
        branch_unit, _ = normalize(branch_ref[rows, :])
        middle = tok_ref[rows, :].astype(F32) + branch_unit * g_mixed
        middle_ref[rows, :] = middle
        mid_unit, _ = normalize(middle)
        normed = (mid_unit * g_hidden).astype(BF16)
        nm_ref[rows, :] = normed
        down = jnp.zeros((256, 640), F32)
        for half in range(2):
            for n in range(2):
                cols = slice(512 * n, 512 * n + 512)
                u = product(normed, wide_w[0, half, :, :, cols].reshape(640, 512))
                upward = product(normed, wide_w[1, half, :, :, cols].reshape(640, 512))
                square = u * u
                t = jnp.tanh(GELU_A * u * (1.0 + GELU_B * square))
                side = 0.5 * (1.0 + t)
                active = u * side
                slope = side + 0.5 * u * (1.0 - t * t) * (GELU_A * (1.0 + 3.0 * GELU_B * square))
                act_ref[half, rows, cols] = active.astype(BF16)
                slope_ref[half, rows, cols] = (slope * upward).astype(BF16)
                hidden = (active * upward).astype(BF16)
                hid_refs[half][rows, cols] = hidden
                mat = down_w[half, 4 * n : 4 * n + 4].reshape(512, 640)
                down = down + product(hidden, mat)
        down_unit, down_factor = normalize(down)
        out_ref[rows, :] = middle + down_unit * g_final
        grad_out = cot_ref[rows, :].astype(F32)
        gain_sum = gain_sum + column_sum(grad_out * down_unit)
        gd_ref[rows, :] = norm_back(grad_out * g_final, down_unit, down_factor).astype(BF16)
    gain_ref[...] = gain_sum
    down_blocks(hid_other_ref, gd_ref, None, other_ref)


def down_blocks(hid_ref, gd_ref, received, ref):
    for n in range(2):
        members = slice(4 * n, 4 * n + 4)
        part = product_lt(hid_ref[:, 512 * n : 512 * n + 512], gd_ref[...]).reshape(4, 8, 16, 640)
        for i in range(8):
            for j in range(5):
                block = part[:, i, :, 128 * j : 128 * j + 128]
                if received is not None:
                    block = block + received[members, 5 * i + j].astype(F32)
                ref[members, 5 * i + j] = block.astype(BF16)


def wide_blocks(nm_ref, grad_ref, received, ref, start):
    for n in range(2):
        part = product_lt(nm_ref[...], grad_ref[:, 512 * n : 512 * n + 512]).reshape(8, 5, 16, 512)
        for i in range(5):
            for j in range(4):
                at = 8 * i + 4 * n + j
                block = part[:, i, :, 128 * j : 128 * j + 128]
                if received is not None:
                    block = block + received[:, at].astype(F32)
                ref[:, start + at] = block.astype(BF16)


def first_sums_kernel(hid_ref, gd_ref, nm_ref, gg_ref, down_received, gate_received, ref):
    down_blocks(hid_ref, gd_ref, down_received, ref)
    wide_blocks(nm_ref, gg_ref, gate_received, ref, 40)


def second_sums_kernel(nm_ref, gu_ref, up_received, out_own, out_received, ref):
    wide_blocks(nm_ref, gu_ref, up_received, ref, 0)
    for at in range(20):
        block = out_own[:, at].astype(F32) + out_received[:, at].astype(F32)
        ref[:, 40 + at] = block.astype(BF16)
    ref[:, 60:64] = jnp.zeros((8, 4, 16, 128), BF16)


def gate_back_kernel(
    sc_ref, act_ref, slope_ref, gd_ref, nm_ref, t0, t1, t2, t3,
    gg_own_ref, gg_other_ref, gu_own_ref, gu_other_ref, gate_other_ref, down_w, down_sems,
):
    for copy in load_down((t0, t1, t2, t3), down_w, sc_ref[1], down_sems):
        copy.wait()
    for half, (gg_ref, gu_ref) in enumerate(((gg_own_ref, gu_own_ref), (gg_other_ref, gu_other_ref))):
        for n in range(2):
            cols = slice(512 * n, 512 * n + 512)
            mat = down_w[half, 4 * n : 4 * n + 4].reshape(512, 640)
            grad_hidden = product_rt(gd_ref[...], mat)
            gg_ref[:, cols] = (grad_hidden * slope_ref[half, :, cols].astype(F32)).astype(BF16)
            gu_ref[:, cols] = (grad_hidden * act_ref[half, :, cols].astype(F32)).astype(BF16)
    wide_blocks(nm_ref, gg_other_ref, None, gate_other_ref, 0)


def middle_back_kernel(
    sc_ref, nm_ref, mixed_ref, cot_ref, gains_ref, branch_ref, middle_ref, gg_own_ref, gg_other_ref, gu_own_ref,
    gu_other_ref, w0, w1, t0, t1, t2, t3,
    up_other_ref, gmid_ref, gmixed_ref, own_ref, other_ref, gain_ref,
    wide_w, out_w, gb_ref, split_ref, wide_sems, out_sems,
):
    core, zl = sc_ref[0], sc_ref[1]
    wide = load_wide((w0, w1), wide_w, zl, wide_sems)
    wide += load_out((t0, t1, t2, t3), out_w, core, zl, out_sems)
    wide_blocks(nm_ref, gu_other_ref, None, up_other_ref, 0)
    for copy in wide:
        copy.wait()
    g_mixed, g_hidden = [gains_ref[i : i + 1, :640] for i in (1, 2)]
    sum_mixed = jnp.zeros((1, 640), F32)
    sum_hidden = jnp.zeros((1, 640), F32)
    for b in range(2):
        rows = slice(256 * b, 256 * b + 256)
        grad_normed = jnp.zeros((256, 640), F32)
        for half, refs in enumerate(((gg_own_ref, gu_own_ref), (gg_other_ref, gu_other_ref))):
            for at, ref in enumerate(refs):
                grad_normed = grad_normed + product_rt(
                    ref[rows, :], wide_w[at, half].reshape(640, 1024)
                )
        mid_unit, mid_factor = normalize(middle_ref[rows, :])
        sum_hidden = sum_hidden + column_sum(grad_normed * mid_unit)
        grad_middle = cot_ref[rows, :].astype(F32) + norm_back(
            grad_normed * g_hidden, mid_unit, mid_factor
        )
        gmid_ref[rows, :] = grad_middle
        branch_unit, branch_factor = normalize(branch_ref[rows, :])
        sum_mixed = sum_mixed + column_sum(grad_middle * branch_unit)
        grad_branch = norm_back(grad_middle * g_mixed, branch_unit, branch_factor).astype(BF16)
        gb_ref[rows, :] = grad_branch
        gmixed_ref[rows, :] = product_rt(grad_branch, out_w[...].reshape(1024, 640)).astype(BF16)
    gain_ref[0:1, :] = sum_mixed
    gain_ref[1:2, :] = sum_hidden
    for n in range(2):
        part = product_lt(mixed_ref[:, 512 * n : 512 * n + 512], gb_ref[...])
        part = part.astype(BF16).reshape(4, 2, 4, 16, 640)
        for c in range(2):
            split_ref[c, 4 * n : 4 * n + 4] = part[:, c]
    for half, ref in ((core, own_ref), (1 - core, other_ref)):
        part = split_ref[half]
        for i in range(4):
            for j in range(5):
                ref[:, i * 5 + j] = part[:, i, :, 128 * j : 128 * j + 128]


def attend_back_kernel(
    q_ref, k_ref, v_ref, p_ref, gm_ref, gq_ref, far_k_ref, far_v_ref, own_k_ref, own_v_ref, dk_ref, dv_ref
):
    dk_ref[...] = jnp.zeros((1024, 256), F32)
    dv_ref[...] = jnp.zeros((1024, 256), F32)
    for b in range(2):
        rows = slice(256 * b, 256 * b + 256)
        keys = slice(256 * b, 256 * b + 768)
        for h in range(HEADS):
            cols = slice(256 * h, 256 * h + 256)
            probs = p_ref[h, b]
            grads = gm_ref[rows, cols]
            weighed = probs.astype(F32)
            grad_probs = product_rt(grads, v_ref[keys, :])
            inner = jnp.sum(weighed * grad_probs, axis=-1, keepdims=True)
            grad_scores = (weighed * (grad_probs - inner)).astype(BF16)
            gq_ref[rows, cols] = product(grad_scores, k_ref[keys, :]) * SCALE
            dk_ref[keys, :] += product_lt(grad_scores, q_ref[rows, cols])
            dv_ref[keys, :] += product_lt(probs, grads)
    far_k_ref[...] = dk_ref[0:512, :].astype(BF16)
    far_v_ref[...] = dv_ref[0:512, :].astype(BF16)
    own_k_ref[...] = dk_ref[512:1024, :]
    own_v_ref[...] = dv_ref[512:1024, :]


def query_back_kernel(gq_ref, raw_ref, cos_ref, sin_ref, gains_ref, e_ref, low_ref, gn_ref, gain_ref):
    cosine, sine = cos_ref[512:1024, :], sin_ref[512:1024, :]
    g_query = gains_ref[4:5, :256]
    total = jnp.zeros((1, 256), F32)
    for h in range(HEADS):
        cols = slice(256 * h, 256 * h + 256)
        turned = rotate(gq_ref[:, cols], cosine, -sine)
        unit, factor = normalize(raw_ref[:, cols])
        total = total + column_sum(turned * unit)
        low_ref[:, cols] = norm_back(turned * g_query, unit, factor).astype(BF16)
    gain_ref[...] = total
    gn_ref[...] = product_rt(
        low_ref[:, 0:512], e_ref[0, :, 0:80, 0:512].reshape(640, 512)
    ) + product_rt(low_ref[:, 512:1024], e_ref[1, :, 0:80, 0:512].reshape(640, 512))


def early_blocks(heads, last, normed_ref, received, ref):
    for grads, at in ((heads, 0), (last, 4)):
        part = product_lt(normed_ref[...], grads).reshape(8, 5, 16, grads.shape[1])
        for i in range(5):
            for j in range(grads.shape[1] // 128):
                block = part[:, i, :, 128 * j : 128 * j + 128]
                if received is not None:
                    block = block + received[:, i * 6 + at + j].astype(F32)
                ref[:, i * 6 + at + j] = block.astype(BF16)


def key_back_kernel(
    sc_ref, normed_ref, low_ref, own_k_ref, own_v_ref, back_k_ref, back_v_ref, raw_ref, cos_ref, sin_ref,
    gains_ref, gk_ref, gv_ref, other_ref, gain_ref,
):
    other = 1 - sc_ref[0]
    cosine, sine = cos_ref[512:1024, :], sin_ref[512:1024, :]
    key_grad = own_k_ref[...] + back_k_ref[...].astype(F32)
    gv_ref[...] = (own_v_ref[...] + back_v_ref[...].astype(F32)).astype(BF16)
    turned = rotate(key_grad, cosine, -sine)
    unit, factor = normalize(raw_ref[:, 1024:1280])
    gain_ref[...] = column_sum(turned * unit)
    gk_ref[...] = norm_back(turned * gains_ref[5:6, :256], unit, factor).astype(BF16)
    last = jnp.where(other == 0, gk_ref[...].astype(F32), gv_ref[...].astype(F32)).astype(BF16)
    heads = low_ref[:, pl.ds(pl.multiple_of(other * 512, 512), 512)]
    early_blocks(heads, last, normed_ref, None, other_ref)


def token_back_kernel(
    tok_ref, gn_ref, gk_ref, gv_ref, gains_ref, e_ref, gmid_ref, gtok_ref, gain_ref
):
    grad_normed = (
        gn_ref[...]
        + product_rt(gk_ref[...], e_ref[0, :, 0:80, 512:768].reshape(640, 256))
        + product_rt(gv_ref[...], e_ref[1, :, 0:80, 512:768].reshape(640, 256))
    )
    unit_in, factor_in = normalize(tok_ref[...].astype(F32))
    gain_ref[...] = column_sum(grad_normed * unit_in)
    gtok_ref[...] = gmid_ref[...] + norm_back(grad_normed * gains_ref[0:1, :640], unit_in, factor_in)


def early_own_kernel(
    sc_ref, normed_ref, low_ref, gk_ref, gv_ref, received, gain_i_ref, gain_b_ref, gain_f_ref, gain_q_ref,
    gain_k_ref, ref, rows_ref,
):
    core = sc_ref[0]
    last = jnp.where(core == 0, gk_ref[...].astype(F32), gv_ref[...].astype(F32)).astype(BF16)
    heads = low_ref[:, pl.ds(pl.multiple_of(core * 512, 512), 512)]
    early_blocks(heads, last, normed_ref, received, ref)
    rows_ref[...] = jnp.zeros((32, 128), F32)
    spans = (
        (gain_i_ref[...], 0, 5),
        (gain_b_ref[0:1, :], 5, 5),
        (gain_b_ref[1:2, :], 10, 5),
        (gain_f_ref[...], 15, 5),
        (gain_q_ref[...], 20, 2),
        (gain_k_ref[...], 22, 2),
    )
    for vector, start, count in spans:
        for j in range(count):
            rows_ref[start + j : start + j + 1, :] = vector[:, 128 * j : 128 * j + 128]
    blocks = rows_ref[...].astype(BF16).reshape(2, 16, 128)
    for f in range(8):
        ref[f, 30:32] = blocks


def unpack_kernel(
    sc_ref, mine_ref, theirs_ref,
    gq_ref, gk_ref, gv_ref, gout_ref, ggate_ref, gup_ref, gdown_ref,
    gain_0, gain_1, gain_2, gain_3, gain_4, gain_5, both_ref,
):
    core = sc_ref[0]
    both_ref[core] = mine_ref[...]
    both_ref[1 - core] = theirs_ref[...]

    def block(c, kind, at):
        base, per = {"first": (0, 10), "second": (160, 8), "early": (288, 4)}[kind]
        start = base + 16 * (at % per)
        return both_ref[c, at // per, start : start + 16, :].astype(F32)

    for c in range(2):
        for i in range(5):
            rows = slice(16 * i, 16 * i + 16)
            for j in range(8):
                cols = slice(256 * j + 128 * c, 256 * j + 128 * c + 128)
                ggate_ref[rows, cols] = block(c, "first", 40 + 8 * i + j)
                gup_ref[rows, cols] = block(c, "second", 8 * i + j)
            for j in range(4):
                gq_ref[rows, 512 * c + 128 * j : 512 * c + 128 * j + 128] = block(c, "early", 6 * i + j)
            for j in range(2):
                (gk_ref, gv_ref)[c][rows, 128 * j : 128 * j + 128] = block(c, "early", 6 * i + 4 + j)
        for i in range(8):
            for j in range(5):
                cols = slice(128 * j, 128 * j + 128)
                gdown_ref[128 * c + 16 * i : 128 * c + 16 * i + 16, cols] = block(c, "first", 5 * i + j)
                if i < 4:
                    gout_ref[64 * c + 16 * i : 64 * c + 16 * i + 16, cols] = block(
                        c, "second", 40 + 5 * i + j
                    )
    rows = jnp.concatenate(
        [block(0, "early", at) + block(1, "early", at) for at in (30, 31)], axis=0
    )
    member = sc_ref[2]
    for i, (start, count, size) in enumerate(
        ((0, 5, 80), (5, 5, 80), (10, 5, 80), (15, 5, 80), (20, 2, 32), (22, 2, 32))
    ):
        line = jnp.concatenate([rows[start + j : start + j + 1, :] for j in range(count)], axis=1)
        line = jnp.broadcast_to(line, (8, 128 * count))
        turned = pltpu.roll(line, lax.rem(128 * count - member * size, 128 * count), 1)
        (gain_0, gain_1, gain_2, gain_3, gain_4, gain_5)[i][...] = turned[0:1, 0:size]


def on_device(
    tokens,
    positions,
    cotangent,
    query_weight,
    key_weight,
    value_weight,
    output_weight,
    gate_weight,
    upward_weight,
    down_weight,
    gain_input,
    gain_mixed,
    gain_hidden,
    gain_final,
    gain_query,
    gain_key,
):
    core = lax.axis_index("core")
    member = lax.axis_index(FSDP)
    scalars = jnp.stack([core, lax.axis_index("zl"), member]).astype(jnp.int32)

    gain_rows = jnp.concatenate(
        [
            jnp.pad(gain, (0, 128 - gain.shape[0]))[None, :]
            for gain in (gain_input, gain_mixed, gain_hidden, gain_final, gain_query, gain_key)
        ]
        + [jnp.zeros((2, 128), BF16)]
    ).astype(F32)
    early_spread = call(
        early_kernel,
        (scalars, query_weight, key_weight, value_weight, output_weight, down_weight, gain_rows),
        [SMEM] + [VMEM] * 6,
        [shape((4, 304, 640), BF16)],
    )[0]
    wide = call(
        late_kernel, (scalars, gate_weight, upward_weight), [SMEM] + [VMEM] * 2, [shape((2, 80, 1024), BF16)]
    )[0]
    prev = passed_along(tokens, 1)
    wide_far = along_z(wide, 1)
    near = along_y(early_spread)
    wide_own = along_y(pair_spread(wide, after(wide_far, (near, prev))))
    early_near, tall_near = near[:, :112], near[:, 112:]
    early_far = along_z(early_near, 3)
    early_parts = (early_near, early_far, swapped(early_near), swapped(early_far))
    tall_far = along_z(tall_near, 1)
    tall_parts = (tall_near, tall_far, swapped(tall_near), swapped(tall_far))

    before = positions[0] - ROWS + jnp.arange(ROWS, dtype=jnp.int32)
    freqs = THETA ** (-(jnp.arange(HEAD // 2, dtype=F32) * 2.0) / HEAD)
    phase = jnp.concatenate([before, positions]).astype(F32)[:, None] * freqs[None, :]
    cosine, sine = jnp.cos(phase), jnp.sin(phase)

    queries, keys, values, raw, probs, mixed, gains, normed, mats = call(
        attend_kernel,
        (scalars, tokens, prev, cosine, sine, positions[:, None]) + early_parts,
        [SMEM] + [VMEM] * 5 + [ANY] * 4,
        [
            shape((512, 1024), BF16),
            shape((1024, 256), BF16),
            shape((1024, 256), BF16),
            shape((512, 1280), F32),
            shape((4, 2, 256, 768), BF16),
            shape((512, 1024), BF16),
            shape((16, 640), F32),
            shape((512, 640), BF16),
            shape((2, 8, 96, 768), BF16),
        ],
        [pltpu.SemaphoreType.DMA((28,))],
        us=9,
    )
    wide_own = after(wide_own, (mixed,) + tall_parts)
    wide_parts = (wide_own, swapped(wide_own))
    wide_scratch = pltpu.VMEM((2, 2, 8, 80, 1024), BF16)
    out_scratch = pltpu.VMEM((8, 2, 64, 640), BF16)
    down_scratch = pltpu.VMEM((2, 8, 128, 640), BF16)
    sems_4, sems_8 = pltpu.SemaphoreType.DMA((4,)), pltpu.SemaphoreType.DMA((8,))
    layer_out, branch, middle, normed_mid, active, slope, grad_down, hid_own, down_other, gain_f = call(
        forward_kernel,
        (scalars, mixed, tokens, cotangent, gains) + wide_parts + tall_parts,
        [SMEM] + [VMEM] * 4 + [ANY] * 6,
        [
            shape((512, 640), F32),
            shape((512, 640), F32),
            shape((512, 640), F32),
            shape((512, 640), BF16),
            shape((2, 512, 1024), BF16),
            shape((2, 512, 1024), BF16),
            shape((512, 640), BF16),
            shape((512, 1024), BF16),
            shape((8, 40, 16, 128), BF16),
            shape((1, 640), F32),
        ],
        [wide_scratch, out_scratch, down_scratch, pltpu.VMEM((512, 1024), BF16), sems_8, sems_4, sems_4],
        us=13,
    )
    down_received = swapped(down_other)
    half = shape((512, 1024), BF16)
    blocks = shape((8, 40, 16, 128), BF16)
    gg_own, gg_other, gu_own, gu_other, gate_other = call(
        gate_back_kernel,
        (scalars, active, slope, grad_down, normed_mid) + tall_parts,
        [SMEM] + [VMEM] * 4 + [ANY] * 4,
        [half, half, half, half, blocks],
        [down_scratch, sems_4],
        us=8,
    )
    first_sum = call(
        first_sums_kernel,
        (hid_own, grad_down, normed_mid, gg_own, down_received, swapped(gate_other)),
        [VMEM] * 6,
        [shape((8, 80, 16, 128), BF16)],
        us=6,
    )[0]
    first_part = chips_sum(first_sum.reshape(64, 160, 128))
    up_other, grad_middle, grad_mixed, out_own, out_other, gain_b = call(
        middle_back_kernel,
        (
            scalars, after(normed_mid, first_sum), mixed, cotangent, gains, branch, middle, gg_own, gg_other,
            gu_own, gu_other,
        )
        + wide_parts
        + tall_parts,
        [SMEM] + [VMEM] * 10 + [ANY] * 6,
        [
            blocks,
            shape((512, 640), F32),
            shape((512, 1024), BF16),
            shape((8, 20, 16, 128), BF16),
            shape((8, 20, 16, 128), BF16),
            shape((2, 640), F32),
        ],
        [
            wide_scratch,
            out_scratch,
            pltpu.VMEM((512, 640), BF16),
            pltpu.VMEM((2, 8, 4, 16, 640), BF16),
            sems_8,
            sems_4,
        ],
        us=13,
    )
    grad_queries, far_k, far_v, own_k, own_v = call(
        attend_back_kernel,
        (queries, keys, values, probs, grad_mixed),
        [VMEM] * 5,
        [
            shape((512, 1024), F32),
            shape((512, 256), BF16),
            shape((512, 256), BF16),
            shape((512, 256), F32),
            shape((512, 256), F32),
        ],
        [pltpu.VMEM((1024, 256), F32), pltpu.VMEM((1024, 256), F32)],
        us=6,
    )
    back_k = passed_along(far_k, -1)
    back_v = passed_along(far_v, -1)
    second_sum = call(
        second_sums_kernel,
        (after(normed_mid, far_k), gu_own, swapped(up_other), out_own, swapped(out_other)),
        [VMEM] * 5,
        [shape((8, 64, 16, 128), BF16)],
        us=4,
    )[0]
    second_part = chips_sum(after(second_sum.reshape(64, 128, 128), (first_part, back_k, back_v)))
    low_query, grad_normed, gain_q = call(
        query_back_kernel,
        (grad_queries, raw, cosine, sine, gains, mats),
        [VMEM] * 6,
        [shape((512, 1024), BF16), shape((512, 640), F32), shape((1, 256), F32)],
    )
    small = shape((512, 256), BF16)
    grad_key, grad_value, early_other, gain_k = call(
        key_back_kernel,
        (scalars, normed, low_query, own_k, own_v, back_k, back_v, raw, cosine, sine, gains),
        [SMEM] + [VMEM] * 10,
        [small, small, shape((8, 30, 16, 128), BF16), shape((1, 256), F32)],
    )
    early_received = swapped(early_other)
    grad_tokens, gain_i = call(
        token_back_kernel,
        (tokens, grad_normed, grad_key, grad_value, gains, mats, grad_middle),
        [VMEM] * 7,
        [shape((512, 640), F32), shape((1, 640), F32)],
    )
    early_sum = call(
        early_own_kernel,
        (
            scalars, normed, low_query, grad_key, grad_value, early_received, gain_i, gain_b, gain_f, gain_q,
            gain_k,
        ),
        [SMEM] + [VMEM] * 10,
        [shape((8, 32, 16, 128), BF16)],
        [pltpu.VMEM((32, 128), F32)],
    )[0]
    early_part = chips_sum(after(early_sum.reshape(64, 64, 128), second_part))
    part = jnp.concatenate([first_part, second_part, early_part], axis=0)
    mine_all = lax.all_to_all(
        jnp.broadcast_to(part[None], (8, 352, 128)), ("x", "zh"), 0, 0, tiled=True
    )
    theirs_all = swapped(mine_all)
    grads = call(
        unpack_kernel,
        (scalars, mine_all, theirs_all),
        [SMEM, VMEM, VMEM],
        [
            shape((80, 1024), F32),
            shape((80, 256), F32),
            shape((80, 256), F32),
            shape((128, 640), F32),
            shape((80, 2048), F32),
            shape((80, 2048), F32),
            shape((256, 640), F32),
            *[shape((1, size), F32) for size in (80, 80, 80, 80, 32, 32)],
        ],
        [pltpu.VMEM((2, 8, 352, 128), BF16)],
    )
    gain_grads = [grad.reshape(-1) for grad in grads[7:]]
    return (layer_out, grad_tokens, *grads[:7], *gain_grads)


def solution(mesh):
    fine = Mesh(mesh.devices.reshape(4, 2, 2, 2, 4), REP + FSDP)
    rows = P(REP + FSDP, None)
    weight = P(FSDP, None)
    gain = P(FSDP)
    in_specs = (rows, P(REP + FSDP), rows) + (weight,) * 7 + (gain,) * 6
    out_specs = (rows, rows) + (weight,) * 7 + (gain,) * 6
    return jax.shard_map(
        on_device, mesh=fine, in_specs=in_specs, out_specs=out_specs, check_vma=False
    )
```
